32 devices in a mesh: groups: 2 (over y), seq: 16 (over z, x, core).
Axes of the slice: x: 2, y: 2, z: 4, core: 2. Of those that a mesh axis runs over, the one named last changes fastest.
Arguments:
- tokens: bfloat16 [4096, 256], P(('groups', 'seq')), parts along dimension 0, may hold values from -6 to 6
- inv_rms_a: float32 [4096], P(('groups', 'seq')), parts along dimension 0, may hold values from 0.5 to 2
- gain_a: float32 [256], replicated, may hold values from 0.1 to 1.9
- proj_a: bfloat16 [256, 768], replicated, may hold values from -0.375 to 0.375
- taps_a: bfloat16 [128, 256], replicated, may hold values from -0.5 to 0.5
- out_a: bfloat16 [256, 256], replicated, may hold values from -0.375 to 0.375
- inv_rms_b: float32 [4096], P(('groups', 'seq')), parts along dimension 0, may hold values from 0.5 to 2
- gain_b: float32 [256], replicated, may hold values from 0.1 to 1.9
- proj_b: bfloat16 [256, 768], replicated, may hold values from -0.375 to 0.375
- rates_b: float32 [16, 256], replicated, may hold values from 1.4648438e-06 to 0.033
- residues_b: float32 [16, 256], replicated, may hold values from -4 to 4
- out_b: bfloat16 [256, 256], replicated, may hold values from -0.375 to 0.375
Outputs:
- partial_a: bfloat16 [4096, 256], P(('groups', 'seq')), parts along dimension 0
- partial_b: bfloat16 [4096, 256], P(('groups', 'seq')), parts along dimension 0
The draws below stay inside these ranges and needn't reach their ends.
There are 2 independent parts, one for each index of `groups`. The reference program is written for one: setup_inputs(seed, part) draws one part's arguments, and reference() takes and returns one part's arrays. A program takes and returns all parts, laid end to end along the dimension named above; an argument that names none is the same for every part. Nothing has to cross between parts.
All inputs are finite; a program needn't handle non-finite values.
Results may differ from the reference program's by a relative error of at most 0.019.
Values may be sent and summed in bfloat16 or wider, within the bound.
No kernel may reach another device: no remote copies, remote signals or barrier semaphores. Data moves between devices by JAX's collectives and lax.ppermute only.
A program may use at most 64 MiB of HBM per device.

```python
import math
import jax
import jax.numpy as jnp
from jax import lax

D = 256
TAPS = 128
MODES = 16
TOKENS = 2048


def block_levels(rng, shape, cuts, least, high):
    def one(position, shards_of):
        draws = jax.random.uniform(jax.random.fold_in(jax.random.fold_in(rng, 6), position), (shards_of,), jnp.float32, least / len(cuts), high / len(cuts))
        return jnp.repeat(jnp.exp(draws), shape[position] // shards_of).reshape((-1,) + (1,) * (len(shape) - position - 1))

    level = one(*cuts[0])
    for cut in cuts[1:]:
        level = level * one(*cut)
    return level


def noise(own_key, shape, deviation, most, split=(), kind=jnp.bfloat16):
    result = jax.random.normal(own_key, shape, jnp.float32) * deviation
    if len(split) > 0:
        result = block_levels(own_key, shape, split, -0.22, 0.18) * result
    return jnp.clip(result, min=-most, max=most).astype(kind)


def setup_inputs(seed: int = 0, part: int = 0) -> dict:
    key_list = jax.random.split(jax.random.key(seed), 13)
    part_splits = jax.random.split(jax.random.fold_in(key_list[12], part), 13)
    return {
        "tokens": noise(part_splits[0], (TOKENS, D), 1.0, 6.0, ((0, 16),)),
        "inv_rms_a": jnp.clip(jnp.exp(math.log(2.0) - 1.3862944 * jax.random.uniform(part_splits[1], (TOKENS,), jnp.float32) ** block_levels(part_splits[1], (TOKENS,), ((0, 16),), -0.2, 0.2)), 0.5, 2.0),
        "gain_a": jnp.clip(1.0 + 0.18 * jax.random.normal(key_list[2], (D,), jnp.float32), 0.1, 1.9),
        "proj_a": noise(key_list[3], (D, 3 * D), D ** -0.5, 0.375),
        "taps_a": noise(key_list[4], (TAPS, D), TAPS ** -0.5, 0.5),
        "out_a": noise(key_list[5], (D, D), D ** -0.5, 0.375),
        "inv_rms_b": jnp.clip(jnp.exp(math.log(2.0) - 1.3862944 * jax.random.uniform(part_splits[6], (TOKENS,), jnp.float32) ** block_levels(part_splits[6], (TOKENS,), ((0, 16),), -0.2, 0.2)), 0.5, 2.0),
        "gain_b": jnp.clip(1.0 + 0.18 * jax.random.normal(key_list[7], (D,), jnp.float32), 0.1, 1.9),
        "proj_b": noise(key_list[8], (D, 3 * D), D ** -0.5, 0.375),
        "rates_b": jnp.clip(jnp.exp(jax.random.uniform(key_list[9], (MODES, D), jnp.float32, math.log(1.4648437627329258e-06), math.log(0.033))), 1.4648437627329258e-06, 0.033),
        "residues_b": noise(key_list[10], (MODES, D), 0.3, 4.0, (), jnp.float32),
        "out_b": noise(key_list[11], (D, D), D ** -0.5, 0.375),
    }


HIGHEST_PREC = lax.Precision.HIGHEST

def rms_scale(values, inv_rms, gain):
    floats = values.astype(jnp.float32)
    return (floats * inv_rms[:, None] * gain).astype(jnp.bfloat16)

def mode_weights(rates, residues, length):
    energy = -jnp.expm1(-2.0 * rates) / -jnp.expm1(-2.0 * rates * length)
    return residues * jnp.sqrt(energy)

def long_filter(rates, residues):
    weights = mode_weights(rates, residues, float(TOKENS))
    positions = jnp.arange(TOKENS).astype(jnp.float32)[:, None]

    def add_mode(totals, mode_pair):
        mode_rate, mode_weight = mode_pair
        return (totals + mode_weight[None, :] * jnp.exp(-mode_rate[None, :] * positions), None)
    return lax.scan(add_mode, jnp.zeros((TOKENS, D), jnp.float32), (rates, weights))[0]

def reference(tokens, inv_rms_a, gain_a, proj_a, taps_a, out_a, inv_rms_b, gain_b, proj_b, rates_b, residues_b, out_b):
    normed = rms_scale(tokens, inv_rms_a, gain_a)
    projected = jnp.dot(normed, proj_a, preferred_element_type=jnp.float32)
    queries = projected[:, :D]
    product = (projected[:, D:2 * D] * projected[:, 2 * D:]).astype(jnp.bfloat16)
    kernel = jnp.flip(taps_a.astype(jnp.float32), 0).T[:, None, :]
    signal_in = product.astype(jnp.float32).T[None]
    short_out = lax.conv_general_dilated(signal_in, kernel, (1,), [(TAPS - 1, 0)], dimension_numbers=('NCH', 'OIH', 'NCH'), feature_group_count=D, precision=HIGHEST_PREC)[0].T
    gated_a = (queries * short_out).astype(jnp.bfloat16)
    partial_a = jnp.dot(gated_a, out_a, preferred_element_type=jnp.float32).astype(jnp.bfloat16)
    hidden = (tokens.astype(jnp.float32) + partial_a.astype(jnp.float32)).astype(jnp.bfloat16)
    normed_b = rms_scale(hidden, inv_rms_b, gain_b)
    projected_b = jnp.dot(normed_b, proj_b, preferred_element_type=jnp.float32)
    queries_b = projected_b[:, :D]
    signal = (projected_b[:, D:2 * D] * projected_b[:, 2 * D:]).astype(jnp.bfloat16)
    fft_size = 2 * TOKENS
    spectrum = jnp.fft.rfft(signal.astype(jnp.float32), n=fft_size, axis=0) * jnp.fft.rfft(long_filter(rates_b, residues_b), n=fft_size, axis=0)
    long_out = jnp.fft.irfft(spectrum, n=fft_size, axis=0)[:TOKENS].astype(jnp.bfloat16)
    long_out = lax.optimization_barrier(long_out)
    gated_b = (queries_b * long_out.astype(jnp.float32)).astype(jnp.bfloat16)
    partial_b = jnp.dot(gated_b, out_b, preferred_element_type=jnp.float32).astype(jnp.bfloat16)
    return (partial_a, partial_b)
```

```python
import functools

import jax
import jax.numpy as jnp
from jax import lax
from jax.experimental import pallas as pl
from jax.experimental.pallas import tpu as pltpu
from jax.sharding import PartitionSpec as P

F32 = jnp.float32
BF16 = jnp.bfloat16
LANES = 128
SUB = 8
TAP_GROUP = 4
STEP = SUB * TAP_GROUP
VMEM_LIMIT = 32 * 1024 * 1024


def call(kernel, outs, scratch=(), flops=0, data=0):
    return pl.pallas_call(
        kernel,
        out_shape=outs,
        out_specs=jax.tree.map(lambda _: pl.BlockSpec(memory_space=pltpu.VMEM), outs),
        scratch_shapes=list(scratch),
        compiler_params=pltpu.CompilerParams(vmem_limit_bytes=VMEM_LIMIT),
        cost_estimate=pl.CostEstimate(flops=flops, bytes_accessed=data, transcendentals=0),
    )


def spread(scales, width):
    rows = scales.shape[1]
    square = jnp.transpose(jnp.broadcast_to(scales, (LANES, rows)))
    return jnp.concatenate([square] * (width // LANES), 1)


def scaled(values, scales, gain):
    return (values * spread(scales, values.shape[1]) * gain).astype(BF16)


def dot(left, right):
    return jnp.dot(left, right, preferred_element_type=F32)


def shifted_copies(values, store, lead):
    rows, width = values.shape
    tail = store.shape[1] - lead - rows
    if tail:
        values = jnp.concatenate([values, jnp.zeros((tail, width), F32)], 0)
    if lead:
        values = jnp.concatenate([jnp.zeros((lead, width), F32), values], 0)
    store[0] = values
    for r in range(1, SUB):
        store[r] = pltpu.roll(values, r, 0)


def tap_sum(taps, store, group, base, size):
    width = store.shape[2]

    def body(step, total):
        first = pl.multiple_of(base - step * SUB, SUB)
        for r in range(SUB):
            tap = taps[pl.ds((group * TAP_GROUP + step) * SUB + r, 1), :]
            total = total + tap * store[r, pl.ds(first, size), :]
        return total

    return lax.fori_loop(0, TAP_GROUP, body, jnp.zeros((size, width), F32))


def own_taps(values, taps, store, total):
    rows = values.shape[0]
    shifted_copies(values, store, STEP)
    total[...] = tap_sum(taps, store, 0, STEP, rows)
    for group in range(1, rows // STEP):
        skip = group * STEP
        total[pl.ds(skip, rows - skip), :] += tap_sum(taps, store, group, STEP, rows - skip)


def rim_taps(values, taps, store, total):
    rows = values.shape[0]
    shifted_copies(values, store, 0)
    for group in range(rows // STEP):
        size = (group + 1) * STEP
        total[pl.ds(0, size), :] += tap_sum(taps, store, group, rows - group * STEP, size)


def first_kernel(tokens, inv_rms, gain, proj, queries, product):
    width = tokens.shape[1]
    normed = scaled(tokens[...].astype(F32), inv_rms[...], gain[...])
    projected = dot(normed, proj[...])
    queries[...] = projected[:, :width]
    product[...] = (projected[:, width : 2 * width] * projected[:, 2 * width :]).astype(BF16)


def near_kernel(product, taps, total, store, taps_wide):
    taps_wide[...] = taps[...].astype(F32)
    own_taps(product[...].astype(F32), taps_wide, store, total)


def middle_kernel(
    near, rim, taps, queries, out_a, tokens, inv_rms, gain, proj, fade, fall,
    partial, signal, queries_b, state, store, taps_wide, total,
):
    width = near.shape[1]
    modes = fade.shape[0]
    taps_wide[...] = taps[...].astype(F32)
    total[...] = near[...]
    rim_taps(rim[...].astype(F32), taps_wide, store, total)
    gated = (queries[...] * total[...]).astype(BF16)
    term = dot(gated, out_a[...]).astype(BF16)
    partial[...] = term
    hidden = (tokens[...].astype(F32) + term.astype(F32)).astype(BF16)
    normed = scaled(hidden.astype(F32), inv_rms[...], gain[...])
    pair = dot(normed, proj[:, width:])
    mixed = (pair[:, :width] * pair[:, width:]).astype(BF16).astype(F32)
    signal[...] = mixed
    for lane in range(0, width, LANES):
        here = slice(lane, lane + LANES)
        for m in range(modes):
            drop = fade[m : m + 1, here]
            held = mixed[:SUB, here]
            for row in range(SUB, mixed.shape[0], SUB):
                held = held * drop + mixed[row : row + SUB, here]
            state[m : m + 1, here] = jnp.sum(held * fall[m, :, here], 0, keepdims=True)
    queries_b[...] = dot(normed, proj[:, :width])


def local_kernel(signal, response, total, store):
    own_taps(signal[...], response, store, total)


def last_kernel(near, carry, rise, fade, queries, out_b, partial):
    rows, width = near.shape
    modes = fade.shape[0]
    columns = []
    for lane in range(0, width, LANES):
        here = slice(lane, lane + LANES)
        sums = [near[row : row + SUB, here] for row in range(0, rows, SUB)]
        for m in range(modes):
            drop = fade[m : m + 1, here]
            held = carry[m : m + 1, here] * rise[m, :, here]
            for i in range(len(sums)):
                sums[i] = sums[i] + held
                if i + 1 < len(sums):
                    held = held * drop
        columns.append(jnp.concatenate(sums, 0))
    long_out = jnp.concatenate(columns, 1).astype(BF16).astype(F32)
    gated = (queries[...] * long_out).astype(BF16)
    partial[...] = dot(gated, out_b[...]).astype(BF16)


def mode_weights(rates, residues, length):
    energy = -jnp.expm1(-2.0 * rates) / -jnp.expm1(-2.0 * rates * length)
    return residues * jnp.sqrt(energy)


def levels(devices):
    found, stride = [], 1
    while stride < devices:
        radix = 4 if devices // stride % 4 == 0 else 2
        found.append((stride, radix))
        stride *= radix
    assert stride == devices
    return found


def swap(block, devices, mask):
    return lax.ppermute(block, "seq", [(i, i ^ mask) for i in range(devices)])


def decay(rates, count, keep=True):
    count = jnp.maximum(count, 0).astype(F32)
    return jnp.where(keep, jnp.exp(-rates * count), 0.0)


def states_before(state, rates, rows, devices):
    me = lax.axis_index("seq")
    before = jnp.zeros_like(state)
    total = state
    for stride, radix in levels(devices):
        place = me // stride % radix
        parts = [total] + [swap(total, devices, k * stride) for k in range(1, radix)]
        summed = jnp.zeros_like(state)
        for k, part in enumerate(parts):
            other = place ^ k
            gap = ((place - 1 - other) * stride + me % stride) * rows
            before = before + part * decay(rates, gap, other < place)
            summed = summed + part * decay(rates, (radix - 1 - other) * stride * rows)
        total = summed
    return before


def on_device(
    tokens,
    inv_rms_a,
    gain_a,
    proj_a,
    taps_a,
    out_a,
    inv_rms_b,
    gain_b,
    proj_b,
    rates_b,
    residues_b,
    out_b,
):
    rows, width = tokens.shape
    taps = taps_a.shape[0]
    modes = rates_b.shape[0]
    devices = lax.axis_size("seq")
    assert taps == rows and rows % STEP == 0
    wide = jax.ShapeDtypeStruct((rows, width), F32)
    narrow = jax.ShapeDtypeStruct((rows, width), BF16)
    own_store = pltpu.VMEM((SUB, rows + STEP, width), F32)
    taps_store = pltpu.VMEM((taps, width), F32)

    queries, product = call(first_kernel, (wide, narrow), flops=6 * rows * width * width)(
        tokens, inv_rms_a[None], gain_a[None], proj_a
    )
    rim = lax.ppermute(product, "seq", [(i, i + 1) for i in range(devices - 1)])

    weights = mode_weights(rates_b, residues_b, float(devices * rows))
    near = call(near_kernel, wide, (own_store, taps_store), flops=8 * rows * rows * width)(
        product, taps_a
    )
    place = jnp.arange(rows, dtype=F32)[None, :, None]
    response = jnp.sum(weights[:, None] * jnp.exp(-rates_b[:, None] * place), 0)
    step = jnp.arange(SUB, dtype=F32)[None, :, None]
    rise = jnp.exp(-rates_b[:, None] * step)
    fall = jnp.exp(-rates_b[:, None] * (SUB - 1.0 - step))
    fade = jnp.exp(-rates_b * float(SUB))

    partial_a, signal, queries_b, state = call(
        middle_kernel,
        (narrow, wide, wide, jax.ShapeDtypeStruct((modes, width), F32)),
        (own_store, taps_store, pltpu.VMEM((rows, width), F32)),
        flops=8 * rows * rows * width,
    )(near, rim, taps_a, queries, out_a, tokens, inv_rms_b[None], gain_b[None], proj_b, fade, fall)

    before = states_before(state, rates_b, rows, devices)
    carry = before * (weights * jnp.exp(-rates_b))
    near_b = call(local_kernel, wide, (own_store,), flops=8 * rows * rows * width)(signal, response)
    partial_b = call(last_kernel, narrow, flops=4 * rows * width * width)(
        near_b, carry, rise, fade, queries_b, out_b
    )
    return (partial_a, partial_b)


def solution(mesh):
    placed = (
        P(("groups", "seq"), None),
        P(("groups", "seq")),
        P(),
        P(),
        P(),
        P(),
        P(("groups", "seq")),
        P(),
        P(),
        P(),
        P(),
        P(),
    )
    return jax.shard_map(
        on_device,
        mesh=mesh,
        in_specs=placed,
        out_specs=(P(("groups", "seq"), None), P(("groups", "seq"), None)),
        check_vma=False,
    )
```

```python
import functools

import jax
import jax.numpy as jnp
from jax import lax
from jax.experimental import pallas as pl
from jax.experimental.pallas import tpu as pltpu
from jax.sharding import PartitionSpec as P

F32 = jnp.float32
BF16 = jnp.bfloat16
LANES = 128
SUB = 8
TAP_GROUP = 4
STEP = SUB * TAP_GROUP
VMEM_LIMIT = 32 * 1024 * 1024
WORK = 4 * 1024 * 1024


def call(kernel, outs, scratch, *arrays):
    spaces = [pltpu.HBM if isinstance(a, list) else pltpu.VMEM for a in arrays]
    placed = [
        pltpu.with_memory_space_constraint(a[0], pltpu.HBM) if isinstance(a, list) else a
        for a in arrays
    ]
    return pl.pallas_call(
        kernel,
        out_shape=outs,
        in_specs=[pl.BlockSpec(memory_space=space) for space in spaces],
        out_specs=[pl.BlockSpec(memory_space=out.memory_space) for out in outs],
        scratch_shapes=list(scratch),
        compiler_params=pltpu.CompilerParams(vmem_limit_bytes=VMEM_LIMIT),
        cost_estimate=pl.CostEstimate(flops=0, bytes_accessed=WORK, transcendentals=0),
    )(*placed)


def spread(scales, width):
    rows = scales.shape[1]
    square = jnp.transpose(jnp.broadcast_to(scales, (LANES, rows)))
    return jnp.concatenate([square] * (width // LANES), 1)


def scaled(values, scales, gain):
    return (values * spread(scales, values.shape[1]) * gain).astype(BF16)


def dot(left, right):
    return jnp.dot(left, right, preferred_element_type=F32)


def shifted_copies(values, store, lead):
    rows, width = values.shape
    tail = store.shape[1] - lead - rows
    if tail:
        values = jnp.concatenate([values, jnp.zeros((tail, width), F32)], 0)
    if lead:
        values = jnp.concatenate([jnp.zeros((lead, width), F32), values], 0)
    store[0] = values
    for r in range(1, SUB):
        store[r] = pltpu.roll(values, r, 0)


def tap_sum(taps, store, group, base, size):
    width = store.shape[2]

    def body(step, total):
        first = pl.multiple_of(base - step * SUB, SUB)
        for r in range(SUB):
            tap = taps[pl.ds((group * TAP_GROUP + step) * SUB + r, 1), :]
            total = total + tap * store[r, pl.ds(first, size), :]
        return total

    return lax.fori_loop(0, TAP_GROUP, body, jnp.zeros((size, width), F32))


def own_taps(values, taps, store, total):
    rows = values.shape[0]
    shifted_copies(values, store, STEP)
    total[...] = tap_sum(taps, store, 0, STEP, rows)
    for group in range(1, rows // STEP):
        skip = group * STEP
        total[pl.ds(skip, rows - skip), :] += tap_sum(taps, store, group, STEP, rows - skip)


def rim_taps(values, taps, store, total):
    rows = values.shape[0]
    shifted_copies(values, store, 0)
    for group in range(rows // STEP):
        size = (group + 1) * STEP
        total[pl.ds(0, size), :] += tap_sum(taps, store, group, rows - group * STEP, size)


def fetches(pairs, sems):
    copies = [pltpu.make_async_copy(a, b, sems.at[i]) for i, (a, b) in enumerate(pairs)]
    for copy in copies:
        copy.start()
    return copies


def first_kernel(
    tokens, inv_rms, gain, proj, taps, rates, residues, inv_rms_b, gain_b,
    product, normed, tokens_in, proj_q, taps_in, rates_in, residues_in, inv_rms_b_in, gain_b_in,
    proj_in, inv_rms_in, gain_in, sems,
):
    width = tokens.shape[1]
    copies = fetches(
        [
            (tokens, tokens_in),
            (inv_rms, inv_rms_in),
            (gain, gain_in),
            (proj.at[:, width:], proj_in),
            (proj.at[:, :width], proj_q),
            (taps, taps_in),
            (rates, rates_in),
            (residues, residues_in),
            (inv_rms_b, inv_rms_b_in),
            (gain_b, gain_b_in),
        ],
        sems,
    )
    for copy in copies[:3]:
        copy.wait()
    normed[...] = scaled(tokens_in[...].astype(F32), inv_rms_in[...], gain_in[...])
    copies[3].wait()
    pair = dot(normed[...], proj_in[...])
    product[...] = (pair[:, :width] * pair[:, width:]).astype(BF16)
    for copy in copies[4:]:
        copy.wait()


def near_kernel(
    devices, product, normed, proj_q, taps, rates, residues, inv_rms, gain, out_a, out_b, proj,
    total, queries, taps_wide, scale, weights, rise, fall, fade, shares, out_a_in, out_b_in, proj_in,
    store, sems,
):
    copies = fetches([(out_a, out_a_in), (proj, proj_in), (out_b, out_b_in)], sems)
    rows, width = product.shape
    modes = rates.shape[0]
    taps_wide[...] = taps[...].astype(F32)
    own_taps(product[...].astype(F32), taps_wide, store, total)
    queries[...] = dot(normed[...], proj_q[...])
    scale[...] = spread(inv_rms[...], width) * gain[...]
    rate = rates[...]
    weight = mode_weights(rate, residues[...], float(devices * rows))
    weights[...] = weight
    fade[...] = jnp.exp(rate * -float(SUB))
    step = lax.broadcasted_iota(jnp.int32, (SUB, width), 0).astype(F32)
    for m in range(modes):
        rise[m] = jnp.exp(-rate[m : m + 1] * step)
        fall[m] = jnp.exp(-rate[m : m + 1] * (SUB - 1.0 - step))
    me = lax.axis_index("seq")
    weight = weight * jnp.exp(-rate)
    for i, (last, count, keep) in enumerate(share_plan(me, devices, rows)):
        share = jnp.exp(-rate * jnp.maximum(count, 0).astype(F32))
        if last:
            share = jnp.where(keep, share * weight, 0.0)
        shares[i] = share
    for copy in copies:
        copy.wait()


def middle_kernel(
    near, rim_chain, rim_pair, taps, queries, out_a, tokens, scale, proj, fade, fall,
    partial, signal, normed_b, state, store, total,
):
    width = near.shape[1]
    modes = fade.shape[0]
    me = lax.axis_index("seq")
    total[...] = near[...]
    rim = jnp.where(me % 2 == 1, rim_pair[...].astype(F32), rim_chain[...].astype(F32))
    rim_taps(jnp.where(me == 0, 0.0, rim), taps, store, total)
    gated = (queries[...] * total[...]).astype(BF16)
    term = dot(gated, out_a[...]).astype(BF16)
    partial[...] = term
    hidden = (tokens[...].astype(F32) + term.astype(F32)).astype(BF16)
    normed = (hidden.astype(F32) * scale[...]).astype(BF16)
    normed_b[...] = normed
    pair = dot(normed, proj[:, width:])
    mixed = (pair[:, :width] * pair[:, width:]).astype(BF16).astype(F32)
    signal[...] = mixed
    for lane in range(0, width, LANES):
        here = slice(lane, lane + LANES)
        for m in range(modes):
            drop = fade[m : m + 1, here]
            held = mixed[:SUB, here]
            for row in range(SUB, mixed.shape[0], SUB):
                held = held * drop + mixed[row : row + SUB, here]
            state[m : m + 1, here] = jnp.sum(held * fall[m, :, here], 0, keepdims=True)


def local_kernel(
    signal, weights, rise, fade, normed, proj, partial,
    total, queries, partial_out, response, store, sems,
):
    copies = fetches([(partial, partial_out)], sems)
    rows, width = signal.shape
    modes = fade.shape[0]
    for lane in range(0, width, LANES):
        here = slice(lane, lane + LANES)
        sums = [jnp.zeros((SUB, LANES), F32)] * (rows // SUB)
        for m in range(modes):
            add_fading(sums, weights[m : m + 1, here] * rise[m, :, here], fade[m : m + 1, here])
        for i, part in enumerate(sums):
            response[i * SUB : (i + 1) * SUB, here] = part
    own_taps(signal[...], response, store, total)
    queries[...] = dot(normed[...], proj[:, :width])
    for copy in copies:
        copy.wait()


def add_fading(sums, held, drop):
    for i in range(len(sums)):
        sums[i] = sums[i] + held
        if i + 1 < len(sums):
            held = held * drop


def last_kernel(near, carry, rise, fade, queries, out_b, partial, held, sems):
    rows, width = near.shape
    modes = fade.shape[0]
    columns = []
    for lane in range(0, width, LANES):
        here = slice(lane, lane + LANES)
        sums = [near[row : row + SUB, here] for row in range(0, rows, SUB)]
        for m in range(modes):
            add_fading(sums, carry[m : m + 1, here] * rise[m, :, here], fade[m : m + 1, here])
        columns.append(jnp.concatenate(sums, 0))
    long_out = jnp.concatenate(columns, 1).astype(BF16).astype(F32)
    gated = (queries[...] * long_out).astype(BF16)
    held[...] = dot(gated, out_b[...]).astype(BF16)
    for copy in fetches([(held, partial)], sems):
        copy.wait()


def mode_weights(rates, residues, length):
    energy = one_less_exp(2.0 * rates) / one_less_exp(2.0 * rates * length)
    return residues * jnp.sqrt(energy)


def one_less_exp(value):
    series = jnp.ones_like(value)
    for n in range(9, 1, -1):
        series = 1.0 - value * (1.0 / n) * series
    return jnp.where(value < 0.25, value * series, 1.0 - jnp.exp(-value))


def levels(devices):
    found, stride = [], 1
    while stride < devices:
        radix = 4 if devices // stride % 4 == 0 else 2
        found.append((stride, radix))
        stride *= radix
    assert stride == devices
    return found


def share_plan(me, devices, rows):
    plan = []
    for stride, radix in levels(devices):
        place = me // stride % radix
        for k in range(1, radix):
            other = place ^ k
            gap = ((place - 1 - other) * stride + me % stride) * rows
            plan.append((True, gap, other < place))
        if stride * radix < devices:
            for k in range(radix):
                plan.append((False, (radix - 1 - (place ^ k)) * stride * rows, None))
    return plan


def swap(block, devices, mask):
    return lax.ppermute(block, "seq", [(i, i ^ mask) for i in range(devices)])


def chain(block, devices):
    route = [(i, i + 1) for i in range(1, devices - 1, 2)]
    if devices < 8:
        free = [*range(0, devices, 2), devices - 1]
        route += list(zip(free, [0, *range(1, devices, 2)]))
    else:
        route += [(i, i - 1) for i in range(4, devices - 2, 2)]
        route += [(0, 1), (2, 0), (devices - 2, devices - 1), (devices - 1, devices - 3)]
    return lax.ppermute(block, "seq", route)


def carry_in(state, shares, near, devices):
    before, total, at = 0.0, state, 0
    for stride, radix in levels(devices):
        cross = 1 if stride > 1 else 0
        parts = [total]
        for k in range(radix - 1, 0, -1):
            parts.insert(1, swap(total, devices, k * stride + cross * (k % 2)))
        for k in range(radix - 1, 0, -1):
            before = before + parts[k] * shares[at + k - 1]
        at += radix - 1
        if stride * radix < devices:
            total = sum(parts[k] * shares[at + k] for k in range(radix - 1, -1, -1))
            at += radix
        if stride == 1:
            total, near = lax.optimization_barrier((total, near))
    return before, near


def on_device(
    tokens,
    inv_rms_a,
    gain_a,
    proj_a,
    taps_a,
    out_a,
    inv_rms_b,
    gain_b,
    proj_b,
    rates_b,
    residues_b,
    out_b,
):
    rows, width = tokens.shape
    taps = taps_a.shape[0]
    modes = rates_b.shape[0]
    devices = lax.axis_size("seq")
    assert taps == rows and rows % STEP == 0 and devices > 2
    wide = pltpu.VMEM((rows, width), F32)
    narrow = pltpu.VMEM((rows, width), BF16)
    square = pltpu.VMEM((width, width), BF16)
    bank = pltpu.VMEM((modes, SUB, width), F32)
    states = pltpu.VMEM((modes, width), F32)
    by_token = pltpu.VMEM((1, rows), F32)
    by_channel = pltpu.VMEM((1, width), F32)
    store = pltpu.VMEM((SUB, rows + STEP, width), F32)
    semaphores = pltpu.SemaphoreType.DMA

    product, normed, tokens, proj_q, taps_a, rates, residues, inv_rms, gain = call(
        first_kernel,
        (narrow, narrow, narrow, square, narrow, states, states, by_token, by_channel),
        (pltpu.VMEM((width, 2 * width), BF16), by_token, by_channel, semaphores((10,))),
        [tokens], [inv_rms_a[None]], [gain_a[None]], [proj_a], [taps_a], [rates_b], [residues_b],
        [inv_rms_b[None]], [gain_b[None]],
    )
    rim_chain = chain(product, devices)
    rim_pair = swap(product, devices, 1)

    shares = pltpu.VMEM((len(share_plan(0, devices, rows)), modes, width), F32)
    (
        near, queries, taps_wide, scale, weights, rise, fall, fade, shares, out_a, out_b, proj_b,
    ) = call(
        functools.partial(near_kernel, devices),
        (
            wide, wide, wide, wide, states, bank, bank, states, shares,
            square, square, pltpu.VMEM(proj_b.shape, BF16),
        ),
        (store, semaphores((3,))),
        product, normed, proj_q, taps_a, rates, residues, inv_rms, gain, [out_a], [out_b], [proj_b],
    )

    partial_a, signal, normed_b, state = call(
        middle_kernel, (narrow, wide, narrow, states), (store, wide),
        near, rim_chain, rim_pair, taps_wide, queries, out_a, tokens, scale, proj_b, fade, fall,
    )
    near_b, queries_b, partial_a = call(
        local_kernel,
        (wide, wide, pltpu.HBM((rows, width), BF16)),
        (wide, store, semaphores((1,))),
        signal, weights, rise, fade, normed_b, proj_b, partial_a,
    )
    carry, near_b = carry_in(state, shares, near_b, devices)
    (partial_b,) = call(
        last_kernel, (pltpu.HBM((rows, width), BF16),), (narrow, semaphores((1,))),
        near_b, carry, rise, fade, queries_b, out_b,
    )
    return (partial_a, partial_b)


def solution(mesh):
    placed = (
        P(("groups", "seq"), None),
        P(("groups", "seq")),
        P(),
        P(),
        P(),
        P(),
        P(("groups", "seq")),
        P(),
        P(),
        P(),
        P(),
        P(),
    )
    return jax.shard_map(
        on_device,
        mesh=mesh,
        in_specs=placed,
        out_specs=(P(("groups", "seq"), None), P(("groups", "seq"), None)),
        check_vma=False,
    )
```

```python
import functools

import jax
import jax.numpy as jnp
from jax import lax
from jax.experimental import pallas as pl
from jax.experimental.pallas import tpu as pltpu
from jax.sharding import PartitionSpec as P

F32 = jnp.float32
BF16 = jnp.bfloat16
LANES = 128
SUB = 8
TAP_GROUP = 4
STEP = SUB * TAP_GROUP
VMEM_LIMIT = 32 * 1024 * 1024
WORK = 4 * 1024 * 1024


def call(kernel, outs, scratch, *arrays):
    spaces = [pltpu.HBM if isinstance(a, list) else pltpu.VMEM for a in arrays]
    placed = [
        pltpu.with_memory_space_constraint(a[0], pltpu.HBM) if isinstance(a, list) else a
        for a in arrays
    ]
    return pl.pallas_call(
        kernel,
        out_shape=outs,
        in_specs=[pl.BlockSpec(memory_space=space) for space in spaces],
        out_specs=[pl.BlockSpec(memory_space=out.memory_space) for out in outs],
        scratch_shapes=list(scratch),
        compiler_params=pltpu.CompilerParams(vmem_limit_bytes=VMEM_LIMIT),
        cost_estimate=pl.CostEstimate(flops=0, bytes_accessed=WORK, transcendentals=0),
    )(*placed)


def spread(scales, width):
    rows = scales.shape[1]
    square = jnp.transpose(jnp.broadcast_to(scales, (LANES, rows)))
    return jnp.concatenate([square] * (width // LANES), 1)


def scaled(values, scales, gain):
    return (values * spread(scales, values.shape[1]) * gain).astype(BF16)


def dot(left, right):
    return jnp.dot(left, right, preferred_element_type=F32)


def shifted_copies(values, store, lead):
    rows, width = values.shape
    tail = store.shape[1] - lead - rows
    if tail:
        values = jnp.concatenate([values, jnp.zeros((tail, width), F32)], 0)
    if lead:
        values = jnp.concatenate([jnp.zeros((lead, width), F32), values], 0)
    store[0] = values
    for r in range(1, SUB):
        store[r] = pltpu.roll(values, r, 0)


def tap_sum(taps, store, group, base, size):
    width = store.shape[2]

    def body(step, total):
        first = pl.multiple_of(base - step * SUB, SUB)
        for r in range(SUB):
            tap = taps[pl.ds((group * TAP_GROUP + step) * SUB + r, 1), :]
            total = total + tap * store[r, pl.ds(first, size), :]
        return total

    return lax.fori_loop(0, TAP_GROUP, body, jnp.zeros((size, width), F32))


def own_taps(values, taps, store, total):
    rows = values.shape[0]
    shifted_copies(values, store, STEP)
    total[...] = tap_sum(taps, store, 0, STEP, rows)
    for group in range(1, rows // STEP):
        skip = group * STEP
        total[pl.ds(skip, rows - skip), :] += tap_sum(taps, store, group, STEP, rows - skip)


def rim_taps(values, taps, store, total):
    rows = values.shape[0]
    shifted_copies(values, store, 0)
    for group in range(rows // STEP):
        size = (group + 1) * STEP
        total[pl.ds(0, size), :] += tap_sum(taps, store, group, rows - group * STEP, size)


def fetches(pairs, sems):
    copies = [pltpu.make_async_copy(a, b, sems.at[i]) for i, (a, b) in enumerate(pairs)]
    for copy in copies:
        copy.start()
    return copies


def first_kernel(
    tokens, inv_rms, gain, proj, taps, rates, residues, inv_rms_b, gain_b,
    product, normed, tokens_in, proj_q, taps_in, rates_in, residues_in, inv_rms_b_in, gain_b_in,
    proj_in, inv_rms_in, gain_in, sems,
):
    width = tokens.shape[1]
    copies = fetches(
        [
            (tokens, tokens_in),
            (inv_rms, inv_rms_in),
            (gain, gain_in),
            (proj.at[:, width:], proj_in),
            (proj.at[:, :width], proj_q),
            (taps, taps_in),
            (rates, rates_in),
            (residues, residues_in),
            (inv_rms_b, inv_rms_b_in),
            (gain_b, gain_b_in),
        ],
        sems,
    )
    for copy in copies[:3]:
        copy.wait()
    normed[...] = scaled(tokens_in[...].astype(F32), inv_rms_in[...], gain_in[...])
    copies[3].wait()
    pair = dot(normed[...], proj_in[...])
    product[...] = (pair[:, :width] * pair[:, width:]).astype(BF16)
    for copy in copies[4:]:
        copy.wait()


def near_kernel(
    devices, product, normed, proj_q, taps, rates, residues, inv_rms, gain, out_a, out_b, proj,
    total, queries, taps_wide, scale, weights, rise, fall, fade, shares, out_a_in, out_b_in, proj_in,
    store, sems,
):
    copies = fetches([(out_a, out_a_in), (proj, proj_in), (out_b, out_b_in)], sems)
    rows, width = product.shape
    modes = rates.shape[0]
    taps_wide[...] = taps[...].astype(F32)
    own_taps(product[...].astype(F32), taps_wide, store, total)
    queries[...] = dot(normed[...], proj_q[...])
    scale[...] = spread(inv_rms[...], width) * gain[...]
    rate = rates[...]
    weight = mode_weights(rate, residues[...], float(devices * rows))
    weights[...] = weight
    fade[...] = jnp.exp(rate * -float(SUB))
    step = lax.broadcasted_iota(jnp.int32, (SUB, width), 0).astype(F32)
    for m in range(modes):
        rise[m] = jnp.exp(-rate[m : m + 1] * step)
        fall[m] = jnp.exp(-rate[m : m + 1] * (SUB - 1.0 - step))
    me = lax.axis_index("seq")
    weight = weight * jnp.exp(-rate)
    for i, (weighted, count, keep) in enumerate(share_plan(me, devices, rows)):
        share = jnp.exp(-rate * jnp.maximum(count, 0).astype(F32))
        shares[i] = jnp.where(keep, share * weight if weighted else share, 0.0)
    for copy in copies:
        copy.wait()


def middle_kernel(
    near, rim_chain, rim_pair, taps, queries, out_a, tokens, scale, proj, fade, fall,
    partial, signal, normed_b, state, store, total,
):
    width = near.shape[1]
    modes = fade.shape[0]
    me = lax.axis_index("seq")
    total[...] = near[...]
    rim = jnp.where(me % 2 == 1, rim_pair[...].astype(F32), rim_chain[...].astype(F32))
    rim_taps(jnp.where(me == 0, 0.0, rim), taps, store, total)
    gated = (queries[...] * total[...]).astype(BF16)
    term = dot(gated, out_a[...]).astype(BF16)
    partial[...] = term
    hidden = (tokens[...].astype(F32) + term.astype(F32)).astype(BF16)
    normed = (hidden.astype(F32) * scale[...]).astype(BF16)
    normed_b[...] = normed
    pair = dot(normed, proj[:, width:])
    mixed = (pair[:, :width] * pair[:, width:]).astype(BF16).astype(F32)
    signal[...] = mixed
    for lane in range(0, width, LANES):
        here = slice(lane, lane + LANES)
        for m in range(modes):
            drop = fade[m : m + 1, here]
            held = mixed[:SUB, here]
            for row in range(SUB, mixed.shape[0], SUB):
                held = held * drop + mixed[row : row + SUB, here]
            state[m : m + 1, here] = jnp.sum(held * fall[m, :, here], 0, keepdims=True)


def local_kernel(
    signal, weights, rise, fade, normed, proj, partial,
    total, queries, partial_out, response, store, sems,
):
    copies = fetches([(partial, partial_out)], sems)
    rows, width = signal.shape
    modes = fade.shape[0]
    for lane in range(0, width, LANES):
        here = slice(lane, lane + LANES)
        sums = [jnp.zeros((SUB, LANES), F32)] * (rows // SUB)
        for m in range(modes):
            add_fading(sums, weights[m : m + 1, here] * rise[m, :, here], fade[m : m + 1, here])
        for i, part in enumerate(sums):
            response[i * SUB : (i + 1) * SUB, here] = part
    own_taps(signal[...], response, store, total)
    queries[...] = dot(normed[...], proj[:, :width])
    for copy in copies:
        copy.wait()


def add_fading(sums, held, drop):
    for i in range(len(sums)):
        sums[i] = sums[i] + held
        if i + 1 < len(sums):
            held = held * drop


def last_kernel(near, carry, rise, fade, queries, out_b, partial, held, sems):
    rows, width = near.shape
    modes = fade.shape[0]
    columns = []
    for lane in range(0, width, LANES):
        here = slice(lane, lane + LANES)
        sums = [near[row : row + SUB, here] for row in range(0, rows, SUB)]
        for m in range(modes):
            add_fading(sums, carry[m : m + 1, here] * rise[m, :, here], fade[m : m + 1, here])
        columns.append(jnp.concatenate(sums, 0))
    long_out = jnp.concatenate(columns, 1).astype(BF16).astype(F32)
    gated = (queries[...] * long_out).astype(BF16)
    held[...] = dot(gated, out_b[...]).astype(BF16)
    for copy in fetches([(held, partial)], sems):
        copy.wait()


def mode_weights(rates, residues, length):
    energy = one_less_exp(2.0 * rates) / one_less_exp(2.0 * rates * length)
    return residues * jnp.sqrt(energy)


def one_less_exp(value):
    series = jnp.ones_like(value)
    for n in range(9, 1, -1):
        series = 1.0 - value * (1.0 / n) * series
    return jnp.where(value < 0.25, value * series, 1.0 - jnp.exp(-value))


def levels(devices):
    found, stride = [], 2
    while stride < devices:
        radix = max(r for r in (2, 4, 8) if devices // stride % r == 0)
        found.append((stride, radix))
        stride *= radix
    assert stride == devices
    return found


def routes(radix):
    return [(k + 1, k) for k in range(radix - 2, 0, -2)] + [(1, 1)]


def share_plan(me, devices, rows):
    core = me % 2
    yes = me >= 0
    plan = [(False, (1 - core) * rows, yes), (False, core * rows, yes)]
    for stride, radix in levels(devices):
        place = me // stride % radix
        inner = me % stride // 2 * 2
        last = stride * radix == devices
        for even, odd in routes(radix):
            other = place ^ jnp.where(core == 0, odd, even)
            once = (core == 0) if even == odd else yes
            gap = ((place - 1 - other) * stride + inner) * rows
            plan.append((False, gap, (other < place) & once))
            if not last:
                plan.append((False, (radix - 1 - other) * stride * rows, once))
        if not last:
            plan.append((False, (radix - 1 - place) * stride * rows, core == 0))
    return plan + [(True, core * rows, yes), (True, 0 * core, core == 1)]


def swap(block, devices, mask):
    return lax.ppermute(block, "seq", [(i, i ^ mask) for i in range(devices)])


def chain(block, devices):
    route = [(i, i + 1) for i in range(1, devices - 1, 2)]
    if devices < 8:
        free = [*range(0, devices, 2), devices - 1]
        route += list(zip(free, [0, *range(1, devices, 2)]))
    else:
        route += [(i, i - 1) for i in range(4, devices - 2, 2)]
        route += [(0, 1), (2, 0), (devices - 2, devices - 1), (devices - 1, devices - 3)]
    return lax.ppermute(block, "seq", route)


def cross(block, devices, stride, even, odd):
    masks = (even * stride + 1, odd * stride + 1)
    return lax.ppermute(block, "seq", [(i, i ^ masks[i % 2]) for i in range(devices)])


def carry_in(state, shares, near, devices):
    share = iter([shares[i] for i in range(shares.shape[0])])
    beside = swap(state, devices, 1)
    total = state * next(share) + beside * next(share)
    before = None
    for stride, radix in levels(devices):
        parts = [cross(total, devices, stride, even, odd) for even, odd in routes(radix)]
        last = stride * radix == devices
        sums, totals = [], []
        for part in parts:
            sums.append(part * next(share))
            if not last:
                totals.append(part * next(share))
        half = functools.reduce(jnp.add, sums)
        before = half if before is None else before + half
        if not last:
            half = functools.reduce(jnp.add, totals) + total * next(share)
            total = half + swap(half, devices, 1)
    before, near = lax.optimization_barrier((before, near))
    before = before + swap(before, devices, 1)
    return before * next(share) + beside * next(share), near


def on_device(
    tokens,
    inv_rms_a,
    gain_a,
    proj_a,
    taps_a,
    out_a,
    inv_rms_b,
    gain_b,
    proj_b,
    rates_b,
    residues_b,
    out_b,
):
    rows, width = tokens.shape
    taps = taps_a.shape[0]
    modes = rates_b.shape[0]
    devices = lax.axis_size("seq")
    assert taps == rows and rows % STEP == 0 and devices > 2
    wide = pltpu.VMEM((rows, width), F32)
    narrow = pltpu.VMEM((rows, width), BF16)
    square = pltpu.VMEM((width, width), BF16)
    bank = pltpu.VMEM((modes, SUB, width), F32)
    states = pltpu.VMEM((modes, width), F32)
    by_token = pltpu.VMEM((1, rows), F32)
    by_channel = pltpu.VMEM((1, width), F32)
    store = pltpu.VMEM((SUB, rows + STEP, width), F32)
    semaphores = pltpu.SemaphoreType.DMA

    product, normed, tokens, proj_q, taps_a, rates, residues, inv_rms, gain = call(
        first_kernel,
        (narrow, narrow, narrow, square, narrow, states, states, by_token, by_channel),
        (pltpu.VMEM((width, 2 * width), BF16), by_token, by_channel, semaphores((10,))),
        [tokens], [inv_rms_a[None]], [gain_a[None]], [proj_a], [taps_a], [rates_b], [residues_b],
        [inv_rms_b[None]], [gain_b[None]],
    )
    rim_chain = chain(product, devices)
    rim_pair = swap(product, devices, 1)

    shares = pltpu.VMEM((len(share_plan(0, devices, rows)), modes, width), F32)
    (
        near, queries, taps_wide, scale, weights, rise, fall, fade, shares, out_a, out_b, proj_b,
    ) = call(
        functools.partial(near_kernel, devices),
        (
            wide, wide, wide, wide, states, bank, bank, states, shares,
            square, square, pltpu.VMEM(proj_b.shape, BF16),
        ),
        (store, semaphores((3,))),
        product, normed, proj_q, taps_a, rates, residues, inv_rms, gain, [out_a], [out_b], [proj_b],
    )

    partial_a, signal, normed_b, state = call(
        middle_kernel, (narrow, wide, narrow, states), (store, wide),
        near, rim_chain, rim_pair, taps_wide, queries, out_a, tokens, scale, proj_b, fade, fall,
    )
    near_b, queries_b, partial_a = call(
        local_kernel,
        (wide, wide, pltpu.HBM((rows, width), BF16)),
        (wide, store, semaphores((1,))),
        signal, weights, rise, fade, normed_b, proj_b, partial_a,
    )
    carry, near_b = carry_in(state, shares, near_b, devices)
    (partial_b,) = call(
        last_kernel, (pltpu.HBM((rows, width), BF16),), (narrow, semaphores((1,))),
        near_b, carry, rise, fade, queries_b, out_b,
    )
    return (partial_a, partial_b)


def solution(mesh):
    placed = (
        P(("groups", "seq"), None),
        P(("groups", "seq")),
        P(),
        P(),
        P(),
        P(),
        P(("groups", "seq")),
        P(),
        P(),
        P(),
        P(),
        P(),
    )
    return jax.shard_map(
        on_device,
        mesh=mesh,
        in_specs=placed,
        out_specs=(P(("groups", "seq"), None), P(("groups", "seq"), None)),
        check_vma=False,
    )
```

```python
import functools

import jax
import jax.numpy as jnp
from jax import lax
from jax.experimental import pallas as pl
from jax.experimental.pallas import tpu as pltpu
from jax.sharding import PartitionSpec as P

F32 = jnp.float32
BF16 = jnp.bfloat16
LANES = 128
SUB = 8
TILE_GROUP = 4
VMEM_LIMIT = 32 * 1024 * 1024
WORK = 4 * 1024 * 1024


def call(kernel, outs, scratch, *arrays):
    spaces = [pltpu.HBM if isinstance(a, list) else pltpu.VMEM for a in arrays]
    placed = [
        pltpu.with_memory_space_constraint(a[0], pltpu.HBM) if isinstance(a, list) else a
        for a in arrays
    ]
    return pl.pallas_call(
        kernel,
        out_shape=outs,
        in_specs=[pl.BlockSpec(memory_space=space) for space in spaces],
        out_specs=[pl.BlockSpec(memory_space=out.memory_space) for out in outs],
        scratch_shapes=list(scratch),
        compiler_params=pltpu.CompilerParams(vmem_limit_bytes=VMEM_LIMIT),
        cost_estimate=pl.CostEstimate(flops=0, bytes_accessed=WORK, transcendentals=0),
    )(*placed)


def spread(scales, width):
    rows = scales.shape[1]
    square = jnp.transpose(jnp.broadcast_to(scales, (LANES, rows)))
    return jnp.concatenate([square] * (width // LANES), 1)


def scaled(values, scales, gain):
    return (values * spread(scales, values.shape[1]) * gain).astype(BF16)


def dot(left, right):
    return jnp.dot(left, right, preferred_element_type=F32)


def repeat_rows(taps, wide):
    for j in range(taps.shape[0]):
        wide[j] = jnp.broadcast_to(taps[j : j + 1, :], wide.shape[1:])


def tap_sums(values, wide, total, rim):
    rows, width = values.shape
    tiles = rows // SUB
    row_ids = lax.broadcasted_iota(jnp.int32, (SUB, LANES), 0)
    start = -1 if rim else 0

    def column(at, carried):
        here = pl.ds(pl.multiple_of(at * LANES, LANES), LANES)
        above = None
        for first in range(start, start + tiles, TILE_GROUP):
            places = range(first, min(first + TILE_GROUP, start + tiles))
            sums = {}
            for q in range(tiles):
                used = [a for a in places if (q > a if rim else q <= a)]
                if not used:
                    continue
                taps = [wide[q * SUB + r, :, here] for r in range(SUB)]
                for a in used:
                    tile = (tiles if rim else 0) + a - q
                    value = values[tile * SUB : (tile + 1) * SUB, here]
                    terms = [tap * value for tap in taps]
                    old = sums.get(a)
                    sums[a] = terms if old is None else [x + y for x, y in zip(old, terms)]
            for a in places:
                turned = sums[a][:1]
                turned += [pltpu.roll(sums[a][r], r, 0) for r in range(1, SUB)]
                if a >= 0:
                    add_tile(a, here, turned, above)
                above = turned
        if rim:
            add_tile(tiles - 1, here, None, above)
        return carried

    def add_tile(a, here, turned, above):
        parts = [] if turned is None else turned[:1]
        for r in range(1, SUB):
            low = 0.0 if turned is None else turned[r]
            high = 0.0 if above is None else above[r]
            parts.append(jnp.where(row_ids < r, high, low))
        while len(parts) > 1:
            parts = [functools.reduce(jnp.add, parts[i : i + 2]) for i in range(0, len(parts), 2)]
        total[a * SUB : (a + 1) * SUB, here] += parts[0]

    lax.fori_loop(0, width // LANES, column, 0)


def fetches(pairs, sems):
    copies = [pltpu.make_async_copy(a, b, sems.at[i]) for i, (a, b) in enumerate(pairs)]
    for copy in copies:
        copy.start()
    return copies


def first_kernel(
    tokens, inv_rms, gain, proj, taps, rates, residues, inv_rms_b, gain_b,
    product, normed, tokens_in, proj_q, taps_in, rates_in, residues_in, inv_rms_b_in, gain_b_in,
    proj_in, inv_rms_in, gain_in, sems,
):
    width = tokens.shape[1]
    copies = fetches(
        [
            (tokens, tokens_in),
            (inv_rms, inv_rms_in),
            (gain, gain_in),
            (proj.at[:, width:], proj_in),
            (proj.at[:, :width], proj_q),
            (taps, taps_in),
            (rates, rates_in),
            (residues, residues_in),
            (inv_rms_b, inv_rms_b_in),
            (gain_b, gain_b_in),
        ],
        sems,
    )
    for copy in copies[:3]:
        copy.wait()
    normed[...] = scaled(tokens_in[...].astype(F32), inv_rms_in[...], gain_in[...])
    copies[3].wait()
    pair = dot(normed[...], proj_in[...])
    product[...] = (pair[:, :width] * pair[:, width:]).astype(BF16)
    for copy in copies[4:]:
        copy.wait()


def near_kernel(
    devices, product, normed, proj_q, taps, rates, residues, inv_rms, gain, out_a, out_b, proj,
    total, queries, taps_wide, scale, weights, rise, fall, fade, shares, out_a_in, out_b_in, proj_in,
    values, sems,
):
    copies = fetches([(out_a, out_a_in), (proj, proj_in), (out_b, out_b_in)], sems)
    rows, width = product.shape
    modes = rates.shape[0]
    repeat_rows(taps[...].astype(F32), taps_wide)
    values[...] = product[...].astype(F32)
    total[...] = jnp.zeros_like(total)
    tap_sums(values, taps_wide, total, rim=False)
    queries[...] = dot(normed[...], proj_q[...])
    scale[...] = spread(inv_rms[...], width) * gain[...]
    rate = rates[...]
    weight = mode_weights(rate, residues[...], float(devices * rows))
    weights[...] = weight
    fade[...] = jnp.exp(rate * -float(SUB))
    step = lax.broadcasted_iota(jnp.int32, (SUB, width), 0).astype(F32)
    for m in range(modes):
        rise[m] = jnp.exp(-rate[m : m + 1] * step)
        fall[m] = jnp.exp(-rate[m : m + 1] * (SUB - 1.0 - step))
    me = lax.axis_index("seq")
    weight = weight * jnp.exp(-rate)
    for i, (weighted, count, keep) in enumerate(share_plan(me, devices, rows)):
        share = jnp.exp(-rate * jnp.maximum(count, 0).astype(F32))
        shares[i] = jnp.where(keep, share * weight if weighted else share, 0.0)
    for copy in copies:
        copy.wait()


def middle_kernel(
    near, rim_chain, rim_pair, taps, queries, out_a, tokens, scale, proj, fade, fall,
    partial, signal, normed_b, state, values, total,
):
    width = near.shape[1]
    modes = fade.shape[0]
    me = lax.axis_index("seq")
    total[...] = near[...]
    rim = jnp.where(me % 2 == 1, rim_pair[...].astype(F32), rim_chain[...].astype(F32))
    values[...] = jnp.where(me == 0, 0.0, rim)
    tap_sums(values, taps, total, rim=True)
    gated = (queries[...] * total[...]).astype(BF16)
    term = dot(gated, out_a[...]).astype(BF16)
    partial[...] = term
    hidden = (tokens[...].astype(F32) + term.astype(F32)).astype(BF16)
    normed = (hidden.astype(F32) * scale[...]).astype(BF16)
    normed_b[...] = normed
    pair = dot(normed, proj[:, width:])
    mixed = (pair[:, :width] * pair[:, width:]).astype(BF16).astype(F32)
    signal[...] = mixed
    for lane in range(0, width, LANES):
        here = slice(lane, lane + LANES)
        for m in range(modes):
            drop = fade[m : m + 1, here]
            held = mixed[:SUB, here]
            for row in range(SUB, mixed.shape[0], SUB):
                held = held * drop + mixed[row : row + SUB, here]
            state[m : m + 1, here] = jnp.sum(held * fall[m, :, here], 0, keepdims=True)


def local_kernel(
    signal, weights, rise, fade, normed, proj, partial,
    total, queries, partial_out, response, wide, sems,
):
    copies = fetches([(partial, partial_out)], sems)
    rows, width = signal.shape
    modes = fade.shape[0]
    for lane in range(0, width, LANES):
        here = slice(lane, lane + LANES)
        sums = [jnp.zeros((SUB, LANES), F32)] * (rows // SUB)
        for m in range(modes):
            add_fading(sums, weights[m : m + 1, here] * rise[m, :, here], fade[m : m + 1, here])
        for i, part in enumerate(sums):
            response[i * SUB : (i + 1) * SUB, here] = part
    repeat_rows(response[...], wide)
    total[...] = jnp.zeros_like(total)
    tap_sums(signal, wide, total, rim=False)
    queries[...] = dot(normed[...], proj[:, :width])
    for copy in copies:
        copy.wait()


def add_fading(sums, held, drop):
    for i in range(len(sums)):
        sums[i] = sums[i] + held
        if i + 1 < len(sums):
            held = held * drop


def last_kernel(near, carry, rise, fade, queries, out_b, partial, held, sems):
    rows, width = near.shape
    modes = fade.shape[0]
    columns = []
    for lane in range(0, width, LANES):
        here = slice(lane, lane + LANES)
        sums = [near[row : row + SUB, here] for row in range(0, rows, SUB)]
        for m in range(modes):
            add_fading(sums, carry[m : m + 1, here] * rise[m, :, here], fade[m : m + 1, here])
        columns.append(jnp.concatenate(sums, 0))
    long_out = jnp.concatenate(columns, 1).astype(BF16).astype(F32)
    gated = (queries[...] * long_out).astype(BF16)
    held[...] = dot(gated, out_b[...]).astype(BF16)
    for copy in fetches([(held, partial)], sems):
        copy.wait()


def mode_weights(rates, residues, length):
    energy = one_less_exp(2.0 * rates) / one_less_exp(2.0 * rates * length)
    return residues * jnp.sqrt(energy)


def one_less_exp(value):
    series = jnp.ones_like(value)
    for n in range(9, 1, -1):
        series = 1.0 - value * (1.0 / n) * series
    return jnp.where(value < 0.25, value * series, 1.0 - jnp.exp(-value))


def levels(devices):
    found, stride = [], 2
    while stride < devices:
        radix = max(r for r in (2, 4, 8) if devices // stride % r == 0)
        found.append((stride, radix))
        stride *= radix
    assert stride == devices
    return found


def routes(radix):
    return [(k + 1, k) for k in range(radix - 2, 0, -2)] + [(1, 1)]


def share_plan(me, devices, rows):
    core = me % 2
    yes = me >= 0
    plan = [(False, (1 - core) * rows, yes), (False, core * rows, yes)]
    for stride, radix in levels(devices):
        place = me // stride % radix
        inner = me % stride // 2 * 2
        last = stride * radix == devices
        for even, odd in routes(radix):
            other = place ^ jnp.where(core == 0, odd, even)
            once = (core == 0) if even == odd else yes
            gap = ((place - 1 - other) * stride + inner) * rows
            plan.append((False, gap, (other < place) & once))
            if not last:
                plan.append((False, (radix - 1 - other) * stride * rows, once))
        if not last:
            plan.append((False, (radix - 1 - place) * stride * rows, core == 0))
    return plan + [(True, core * rows, yes), (True, 0 * core, core == 1)]


def swap(block, devices, mask):
    return lax.ppermute(block, "seq", [(i, i ^ mask) for i in range(devices)])


def chain(block, devices):
    route = [(i, i + 1) for i in range(1, devices - 1, 2)]
    if devices < 8:
        free = [*range(0, devices, 2), devices - 1]
        route += list(zip(free, [0, *range(1, devices, 2)]))
    else:
        route += [(i, i - 1) for i in range(4, devices - 2, 2)]
        route += [(0, 1), (2, 0), (devices - 2, devices - 1), (devices - 1, devices - 3)]
    return lax.ppermute(block, "seq", route)


def cross(block, devices, stride, even, odd):
    masks = (even * stride + 1, odd * stride + 1)
    return lax.ppermute(block, "seq", [(i, i ^ masks[i % 2]) for i in range(devices)])


def carry_in(state, shares, near, devices):
    share = iter([shares[i] for i in range(shares.shape[0])])
    beside = swap(state, devices, 1)
    total = state * next(share) + beside * next(share)
    before = None
    for stride, radix in levels(devices):
        parts = [cross(total, devices, stride, even, odd) for even, odd in routes(radix)]
        last = stride * radix == devices
        sums, totals = [], []
        for part in parts:
            sums.append(part * next(share))
            if not last:
                totals.append(part * next(share))
        half = functools.reduce(jnp.add, sums)
        before = half if before is None else before + half
        if not last:
            half = functools.reduce(jnp.add, totals) + total * next(share)
            total = half + swap(half, devices, 1)
    before, near = lax.optimization_barrier((before, near))
    before = before + swap(before, devices, 1)
    return before * next(share) + beside * next(share), near


def on_device(
    tokens,
    inv_rms_a,
    gain_a,
    proj_a,
    taps_a,
    out_a,
    inv_rms_b,
    gain_b,
    proj_b,
    rates_b,
    residues_b,
    out_b,
):
    rows, width = tokens.shape
    taps = taps_a.shape[0]
    modes = rates_b.shape[0]
    devices = lax.axis_size("seq")
    assert taps == rows and rows % SUB == 0 and devices > 2
    wide = pltpu.VMEM((rows, width), F32)
    narrow = pltpu.VMEM((rows, width), BF16)
    square = pltpu.VMEM((width, width), BF16)
    bank = pltpu.VMEM((modes, SUB, width), F32)
    states = pltpu.VMEM((modes, width), F32)
    by_token = pltpu.VMEM((1, rows), F32)
    by_channel = pltpu.VMEM((1, width), F32)
    spread_taps = pltpu.VMEM((taps, SUB, width), F32)
    semaphores = pltpu.SemaphoreType.DMA

    product, normed, tokens, proj_q, taps_a, rates, residues, inv_rms, gain = call(
        first_kernel,
        (narrow, narrow, narrow, square, narrow, states, states, by_token, by_channel),
        (pltpu.VMEM((width, 2 * width), BF16), by_token, by_channel, semaphores((10,))),
        [tokens], [inv_rms_a[None]], [gain_a[None]], [proj_a], [taps_a], [rates_b], [residues_b],
        [inv_rms_b[None]], [gain_b[None]],
    )
    rim_chain = chain(product, devices)
    rim_pair = swap(product, devices, 1)

    shares = pltpu.VMEM((len(share_plan(0, devices, rows)), modes, width), F32)
    (
        near, queries, taps_wide, scale, weights, rise, fall, fade, shares, out_a, out_b, proj_b,
    ) = call(
        functools.partial(near_kernel, devices),
        (
            wide, wide, spread_taps, wide, states, bank, bank, states, shares,
            square, square, pltpu.VMEM(proj_b.shape, BF16),
        ),
        (wide, semaphores((3,))),
        product, normed, proj_q, taps_a, rates, residues, inv_rms, gain, [out_a], [out_b], [proj_b],
    )

    partial_a, signal, normed_b, state = call(
        middle_kernel, (narrow, wide, narrow, states), (wide, wide),
        near, rim_chain, rim_pair, taps_wide, queries, out_a, tokens, scale, proj_b, fade, fall,
    )
    near_b, queries_b, partial_a = call(
        local_kernel,
        (wide, wide, pltpu.HBM((rows, width), BF16)),
        (wide, spread_taps, semaphores((1,))),
        signal, weights, rise, fade, normed_b, proj_b, partial_a,
    )
    carry, near_b = carry_in(state, shares, near_b, devices)
    (partial_b,) = call(
        last_kernel, (pltpu.HBM((rows, width), BF16),), (narrow, semaphores((1,))),
        near_b, carry, rise, fade, queries_b, out_b,
    )
    return (partial_a, partial_b)


def solution(mesh):
    placed = (
        P(("groups", "seq"), None),
        P(("groups", "seq")),
        P(),
        P(),
        P(),
        P(),
        P(("groups", "seq")),
        P(),
        P(),
        P(),
        P(),
        P(),
    )
    return jax.shard_map(
        on_device,
        mesh=mesh,
        in_specs=placed,
        out_specs=(P(("groups", "seq"), None), P(("groups", "seq"), None)),
        check_vma=False,
    )
```

```python
import functools

import jax
import jax.numpy as jnp
from jax import lax
from jax.experimental import pallas as pl
from jax.experimental.pallas import tpu as pltpu
from jax.sharding import PartitionSpec as P

F32 = jnp.float32
BF16 = jnp.bfloat16
LANES = 128
SUB = 8
TILE_GROUP = 4
VMEM_LIMIT = 32 * 1024 * 1024
WORK = 4 * 1024 * 1024


def call(kernel, outs, scratch, *arrays):
    spaces = [pltpu.HBM if isinstance(a, list) else pltpu.VMEM for a in arrays]
    placed = [
        pltpu.with_memory_space_constraint(a[0], pltpu.HBM) if isinstance(a, list) else a
        for a in arrays
    ]
    return pl.pallas_call(
        kernel,
        out_shape=outs,
        in_specs=[pl.BlockSpec(memory_space=space) for space in spaces],
        out_specs=[pl.BlockSpec(memory_space=out.memory_space) for out in outs],
        scratch_shapes=list(scratch),
        compiler_params=pltpu.CompilerParams(vmem_limit_bytes=VMEM_LIMIT),
        cost_estimate=pl.CostEstimate(flops=0, bytes_accessed=WORK, transcendentals=0),
    )(*placed)


def spread(scales, width):
    rows = scales.shape[1]
    square = jnp.transpose(jnp.broadcast_to(scales, (LANES, rows)))
    return jnp.concatenate([square] * (width // LANES), 1)


def scaled(values, scales, gain):
    return (values * spread(scales, values.shape[1]) * gain).astype(BF16)


def dot(left, right):
    return jnp.dot(left, right, preferred_element_type=F32)


def repeat_rows(taps, wide):
    for j in range(taps.shape[0]):
        wide[j] = jnp.broadcast_to(taps[j : j + 1, :], wide.shape[1:])


def tap_sums(values, wide, total, rim):
    rows, width = values.shape
    tiles = rows // SUB
    row_ids = lax.broadcasted_iota(jnp.int32, (SUB, LANES), 0)
    start = -1 if rim else 0

    def column(at, carried):
        here = pl.ds(at * LANES, LANES)
        above = None
        for first in range(start, start + tiles, TILE_GROUP):
            places = range(first, min(first + TILE_GROUP, start + tiles))
            sums = {}
            for q in range(tiles):
                used = [a for a in places if (q > a if rim else q <= a)]
                if not used:
                    continue
                taps = [wide[q * SUB + r, :, here] for r in range(SUB)]
                for a in used:
                    tile = (tiles if rim else 0) + a - q
                    value = values[tile * SUB : (tile + 1) * SUB, here]
                    terms = [tap * value for tap in taps]
                    old = sums.get(a)
                    sums[a] = terms if old is None else [x + y for x, y in zip(old, terms)]
            for a in places:
                turned = sums[a][:1]
                turned += [pltpu.roll(sums[a][r], r, 0) for r in range(1, SUB)]
                if a >= 0:
                    add_tile(a, here, turned, above)
                above = turned
        if rim:
            add_tile(tiles - 1, here, None, above)
        return carried

    def add_tile(a, here, turned, above):
        parts = [] if turned is None else turned[:1]
        for r in range(1, SUB):
            low = 0.0 if turned is None else turned[r]
            high = 0.0 if above is None else above[r]
            parts.append(jnp.where(row_ids < r, high, low))
        while len(parts) > 1:
            parts = [functools.reduce(jnp.add, parts[i : i + 2]) for i in range(0, len(parts), 2)]
        total[a * SUB : (a + 1) * SUB, here] += parts[0]

    for at in range(width // LANES):
        column(at, 0)


def fetches(pairs, sems):
    copies = [pltpu.make_async_copy(a, b, sems.at[i]) for i, (a, b) in enumerate(pairs)]
    for copy in copies:
        copy.start()
    return copies


def first_kernel(
    tokens, inv_rms, gain, proj, taps, rates, residues, inv_rms_b, gain_b,
    product, normed, tokens_in, proj_q, taps_in, rates_in, residues_in, inv_rms_b_in, gain_b_in,
    proj_in, inv_rms_in, gain_in, sems,
):
    width = tokens.shape[1]
    copies = fetches(
        [
            (tokens, tokens_in),
            (inv_rms, inv_rms_in),
            (gain, gain_in),
            (proj.at[:, width:], proj_in),
            (proj.at[:, :width], proj_q),
            (taps, taps_in),
            (rates, rates_in),
            (residues, residues_in),
            (inv_rms_b, inv_rms_b_in),
            (gain_b, gain_b_in),
        ],
        sems,
    )
    for copy in copies[:3]:
        copy.wait()
    normed[...] = scaled(tokens_in[...].astype(F32), inv_rms_in[...], gain_in[...])
    copies[3].wait()
    pair = dot(normed[...], proj_in[...])
    product[...] = (pair[:, :width] * pair[:, width:]).astype(BF16)
    for copy in copies[4:]:
        copy.wait()


def near_kernel(
    devices, product, normed, proj_q, taps, rates, residues, inv_rms, gain, out_a, out_b, proj,
    total, queries, taps_wide, scale, weights, rise, fall, fade, shares, out_a_in, out_b_in, proj_in,
    values, sems,
):
    copies = fetches([(out_a, out_a_in), (proj, proj_in), (out_b, out_b_in)], sems)
    rows, width = product.shape
    modes = rates.shape[0]
    repeat_rows(taps[...].astype(F32), taps_wide)
    values[...] = product[...].astype(F32)
    total[...] = jnp.zeros_like(total)
    tap_sums(values, taps_wide, total, rim=False)
    queries[...] = dot(normed[...], proj_q[...])
    scale[...] = spread(inv_rms[...], width) * gain[...]
    rate = rates[...]
    weight = mode_weights(rate, residues[...], float(devices * rows))
    weights[...] = weight
    fade[...] = jnp.exp(rate * -float(SUB))
    step = lax.broadcasted_iota(jnp.int32, (SUB, width), 0).astype(F32)
    for m in range(modes):
        rise[m] = jnp.exp(-rate[m : m + 1] * step)
        fall[m] = jnp.exp(-rate[m : m + 1] * (SUB - 1.0 - step))
    me = lax.axis_index("seq")
    weight = weight * jnp.exp(-rate)
    for i, (weighted, count, keep) in enumerate(share_plan(me, devices, rows)):
        share = jnp.exp(-rate * jnp.maximum(count, 0).astype(F32))
        shares[i] = jnp.where(keep, share * weight if weighted else share, 0.0)
    for copy in copies:
        copy.wait()


def middle_kernel(
    near, rim_chain, rim_pair, taps, queries, out_a, tokens, scale, proj, fade, fall,
    partial, signal, normed_b, state, values, total,
):
    width = near.shape[1]
    modes = fade.shape[0]
    me = lax.axis_index("seq")
    total[...] = near[...]
    rim = jnp.where(me % 2 == 1, rim_pair[...].astype(F32), rim_chain[...].astype(F32))
    values[...] = jnp.where(me == 0, 0.0, rim)
    tap_sums(values, taps, total, rim=True)
    gated = (queries[...] * total[...]).astype(BF16)
    term = dot(gated, out_a[...]).astype(BF16)
    partial[...] = term
    hidden = (tokens[...].astype(F32) + term.astype(F32)).astype(BF16)
    normed = (hidden.astype(F32) * scale[...]).astype(BF16)
    normed_b[...] = normed
    pair = dot(normed, proj[:, width:])
    mixed = (pair[:, :width] * pair[:, width:]).astype(BF16).astype(F32)
    signal[...] = mixed
    for lane in range(0, width, LANES):
        here = slice(lane, lane + LANES)
        for m in range(modes):
            drop = fade[m : m + 1, here]
            held = mixed[:SUB, here]
            for row in range(SUB, mixed.shape[0], SUB):
                held = held * drop + mixed[row : row + SUB, here]
            state[m : m + 1, here] = jnp.sum(held * fall[m, :, here], 0, keepdims=True)


def local_kernel(
    signal, weights, rise, fade, normed, proj, partial,
    total, queries, partial_out, response, wide, sems,
):
    copies = fetches([(partial, partial_out)], sems)
    rows, width = signal.shape
    modes = fade.shape[0]
    for lane in range(0, width, LANES):
        here = slice(lane, lane + LANES)
        sums = [jnp.zeros((SUB, LANES), F32)] * (rows // SUB)
        for m in range(modes):
            add_fading(sums, weights[m : m + 1, here] * rise[m, :, here], fade[m : m + 1, here])
        for i, part in enumerate(sums):
            response[i * SUB : (i + 1) * SUB, here] = part
    repeat_rows(response[...], wide)
    total[...] = jnp.zeros_like(total)
    tap_sums(signal, wide, total, rim=False)
    queries[...] = dot(normed[...], proj[:, :width])
    for copy in copies:
        copy.wait()


def add_fading(sums, held, drop):
    for i in range(len(sums)):
        sums[i] = sums[i] + held
        if i + 1 < len(sums):
            held = held * drop


def last_kernel(near, carry, rise, fade, queries, out_b, partial, held, sems):
    rows, width = near.shape
    modes = fade.shape[0]
    columns = []
    for lane in range(0, width, LANES):
        here = slice(lane, lane + LANES)
        sums = [near[row : row + SUB, here] for row in range(0, rows, SUB)]
        for m in range(modes):
            add_fading(sums, carry[m : m + 1, here] * rise[m, :, here], fade[m : m + 1, here])
        columns.append(jnp.concatenate(sums, 0))
    long_out = jnp.concatenate(columns, 1).astype(BF16).astype(F32)
    gated = (queries[...] * long_out).astype(BF16)
    held[...] = dot(gated, out_b[...]).astype(BF16)
    for copy in fetches([(held, partial)], sems):
        copy.wait()


def mode_weights(rates, residues, length):
    energy = one_less_exp(2.0 * rates) / one_less_exp(2.0 * rates * length)
    return residues * jnp.sqrt(energy)


def one_less_exp(value):
    series = jnp.ones_like(value)
    for n in range(9, 1, -1):
        series = 1.0 - value * (1.0 / n) * series
    return jnp.where(value < 0.25, value * series, 1.0 - jnp.exp(-value))


def levels(devices):
    found, stride = [], 2
    while stride < devices:
        radix = max(r for r in (2, 4, 8) if devices // stride % r == 0)
        found.append((stride, radix))
        stride *= radix
    assert stride == devices
    return found


def routes(radix):
    pairs = {8: [(5, 4), (7, 6), (3, 2)], 4: [(3, 2)], 2: []}
    return pairs[radix] + [(1, 1)]


def share_plan(me, devices, rows):
    core = me % 2
    yes = me >= 0
    plan = [(False, (1 - core) * rows, yes), (False, core * rows, yes)]
    for stride, radix in levels(devices):
        place = me // stride % radix
        inner = me % stride // 2 * 2
        last = stride * radix == devices
        for even, odd in routes(radix):
            other = place ^ jnp.where(core == 0, odd, even)
            once = (core == 0) if even == odd else yes
            gap = ((place - 1 - other) * stride + inner) * rows
            plan.append((False, gap, (other < place) & once))
            if not last:
                plan.append((False, (radix - 1 - other) * stride * rows, once))
        if not last:
            plan.append((False, (radix - 1 - place) * stride * rows, core == 0))
    return plan + [(True, core * rows, yes), (True, 0 * core, core == 1)]


def swap(block, devices, mask):
    return lax.ppermute(block, "seq", [(i, i ^ mask) for i in range(devices)])


def chain(block, devices):
    route = [(i, i + 1) for i in range(1, devices - 1, 2)]
    if devices < 8:
        free = [*range(0, devices, 2), devices - 1]
        route += list(zip(free, [0, *range(1, devices, 2)]))
    else:
        route += [(i, i - 1) for i in range(4, devices - 2, 2)]
        route += [(0, 1), (2, 0), (devices - 2, devices - 1), (devices - 1, devices - 3)]
    return lax.ppermute(block, "seq", route)


def cross(block, devices, stride, radix, even, odd):
    route = []
    for i in range(devices):
        mask = (even, odd)[i % 2]
        place = i // stride % radix
        short = stride * radix == devices and mask & 6 == 6 and place & 4
        route.append((i, i ^ ((mask ^ 2 if short else mask) * stride + 1)))
    return lax.ppermute(block, "seq", route)


def carry_in(state, shares, near, devices):
    share = iter([shares[i] for i in range(shares.shape[0])])
    beside = swap(state, devices, 1)
    total = state * next(share) + beside * next(share)
    before = None
    for stride, radix in levels(devices):
        parts = [cross(total, devices, stride, radix, even, odd) for even, odd in routes(radix)]
        last = stride * radix == devices
        sums, totals = [], []
        for part in parts:
            sums.append(part * next(share))
            if not last:
                totals.append(part * next(share))
        half = functools.reduce(jnp.add, sums)
        before = half if before is None else before + half
        if not last:
            half = functools.reduce(jnp.add, totals) + total * next(share)
            total = half + swap(half, devices, 1)
    before, near = lax.optimization_barrier((before, near))
    before = before + swap(before, devices, 1)
    return before * next(share) + beside * next(share), near


def on_device(
    tokens,
    inv_rms_a,
    gain_a,
    proj_a,
    taps_a,
    out_a,
    inv_rms_b,
    gain_b,
    proj_b,
    rates_b,
    residues_b,
    out_b,
):
    rows, width = tokens.shape
    taps = taps_a.shape[0]
    modes = rates_b.shape[0]
    devices = lax.axis_size("seq")
    assert taps == rows and rows % SUB == 0 and devices > 2
    wide = pltpu.VMEM((rows, width), F32)
    narrow = pltpu.VMEM((rows, width), BF16)
    square = pltpu.VMEM((width, width), BF16)
    bank = pltpu.VMEM((modes, SUB, width), F32)
    states = pltpu.VMEM((modes, width), F32)
    by_token = pltpu.VMEM((1, rows), F32)
    by_channel = pltpu.VMEM((1, width), F32)
    spread_taps = pltpu.VMEM((taps, SUB, width), F32)
    semaphores = pltpu.SemaphoreType.DMA

    product, normed, tokens, proj_q, taps_a, rates, residues, inv_rms, gain = call(
        first_kernel,
        (narrow, narrow, narrow, square, narrow, states, states, by_token, by_channel),
        (pltpu.VMEM((width, 2 * width), BF16), by_token, by_channel, semaphores((10,))),
        [tokens], [inv_rms_a[None]], [gain_a[None]], [proj_a], [taps_a], [rates_b], [residues_b],
        [inv_rms_b[None]], [gain_b[None]],
    )
    rim_chain = chain(product, devices)
    rim_pair = swap(product, devices, 1)

    shares = pltpu.VMEM((len(share_plan(0, devices, rows)), modes, width), F32)
    (
        near, queries, taps_wide, scale, weights, rise, fall, fade, shares, out_a, out_b, proj_b,
    ) = call(
        functools.partial(near_kernel, devices),
        (
            wide, wide, spread_taps, wide, states, bank, bank, states, shares,
            square, square, pltpu.VMEM(proj_b.shape, BF16),
        ),
        (wide, semaphores((3,))),
        product, normed, proj_q, taps_a, rates, residues, inv_rms, gain, [out_a], [out_b], [proj_b],
    )

    partial_a, signal, normed_b, state = call(
        middle_kernel, (narrow, wide, narrow, states), (wide, wide),
        near, rim_chain, rim_pair, taps_wide, queries, out_a, tokens, scale, proj_b, fade, fall,
    )
    near_b, queries_b, partial_a = call(
        local_kernel,
        (wide, wide, pltpu.HBM((rows, width), BF16)),
        (wide, spread_taps, semaphores((1,))),
        signal, weights, rise, fade, normed_b, proj_b, partial_a,
    )
    carry, near_b = carry_in(state, shares, near_b, devices)
    (partial_b,) = call(
        last_kernel, (pltpu.HBM((rows, width), BF16),), (narrow, semaphores((1,))),
        near_b, carry, rise, fade, queries_b, out_b,
    )
    return (partial_a, partial_b)


def solution(mesh):
    placed = (
        P(("groups", "seq"), None),
        P(("groups", "seq")),
        P(),
        P(),
        P(),
        P(),
        P(("groups", "seq")),
        P(),
        P(),
        P(),
        P(),
        P(),
    )
    return jax.shard_map(
        on_device,
        mesh=mesh,
        in_specs=placed,
        out_specs=(P(("groups", "seq"), None), P(("groups", "seq"), None)),
        check_vma=False,
    )
```

```python
import functools

import jax
import jax.numpy as jnp
from jax import lax
from jax.experimental import pallas as pl
from jax.experimental.pallas import tpu as pltpu
from jax.sharding import PartitionSpec as P

F32 = jnp.float32
BF16 = jnp.bfloat16
LANES = 128
SUB = 8
TILE_GROUP = 4
VMEM_LIMIT = 32 * 1024 * 1024
WORK = 4 * 1024 * 1024


def call(kernel, outs, scratch, *arrays):
    spaces = [pltpu.HBM if isinstance(a, list) else pltpu.VMEM for a in arrays]
    placed = [
        pltpu.with_memory_space_constraint(a[0], pltpu.HBM) if isinstance(a, list) else a
        for a in arrays
    ]
    return pl.pallas_call(
        kernel,
        out_shape=outs,
        in_specs=[pl.BlockSpec(memory_space=space) for space in spaces],
        out_specs=[pl.BlockSpec(memory_space=out.memory_space) for out in outs],
        scratch_shapes=list(scratch),
        compiler_params=pltpu.CompilerParams(vmem_limit_bytes=VMEM_LIMIT),
        cost_estimate=pl.CostEstimate(flops=0, bytes_accessed=WORK, transcendentals=0),
    )(*placed)


def spread(scales, width):
    rows = scales.shape[1]
    square = jnp.transpose(jnp.broadcast_to(scales, (LANES, rows)))
    return jnp.concatenate([square] * (width // LANES), 1)


def scaled(values, scales, gain):
    return (values * spread(scales, values.shape[1]) * gain).astype(BF16)


def dot(left, right):
    return jnp.dot(left, right, preferred_element_type=F32)


def repeat_rows(taps, wide):
    for j in range(taps.shape[0]):
        wide[j] = jnp.broadcast_to(taps[j : j + 1, :], wide.shape[1:])


def tap_sums(values, wide, total, rim):
    rows, width = values.shape
    tiles = rows // SUB
    row_ids = lax.broadcasted_iota(jnp.int32, (SUB, LANES), 0)
    start = -1 if rim else 0

    def column(at, carried):
        here = pl.ds(at * LANES, LANES)
        above = None
        for first in range(start, start + tiles, TILE_GROUP):
            places = range(first, min(first + TILE_GROUP, start + tiles))
            sums = {}
            for q in range(tiles):
                used = [a for a in places if (q > a if rim else q <= a)]
                if not used:
                    continue
                taps = [wide[q * SUB + r, :, here] for r in range(SUB)]
                for a in used:
                    tile = (tiles if rim else 0) + a - q
                    value = values[tile * SUB : (tile + 1) * SUB, here]
                    terms = [tap * value for tap in taps]
                    old = sums.get(a)
                    sums[a] = terms if old is None else [x + y for x, y in zip(old, terms)]
            for a in places:
                turned = sums[a][:1]
                turned += [pltpu.roll(sums[a][r], r, 0) for r in range(1, SUB)]
                if a >= 0:
                    add_tile(a, here, turned, above)
                above = turned
        if rim:
            add_tile(tiles - 1, here, None, above)
        return carried

    def add_tile(a, here, turned, above):
        parts = [] if turned is None else turned[:1]
        for r in range(1, SUB):
            low = 0.0 if turned is None else turned[r]
            high = 0.0 if above is None else above[r]
            parts.append(jnp.where(row_ids < r, high, low))
        while len(parts) > 1:
            parts = [functools.reduce(jnp.add, parts[i : i + 2]) for i in range(0, len(parts), 2)]
        total[a * SUB : (a + 1) * SUB, here] += parts[0]

    for at in range(width // LANES):
        column(at, 0)


def fetches(pairs, sems):
    copies = [pltpu.make_async_copy(a, b, sems.at[i]) for i, (a, b) in enumerate(pairs)]
    for copy in copies:
        copy.start()
    return copies


def first_kernel(
    tokens, inv_rms, gain, proj, taps, product, normed, tokens_in, taps_in,
    proj_in, inv_rms_in, gain_in, sems,
):
    width = tokens.shape[1]
    copies = fetches(
        [
            (tokens, tokens_in),
            (inv_rms, inv_rms_in),
            (gain, gain_in),
            (proj.at[:, width:], proj_in),
            (taps, taps_in),
        ],
        sems,
    )
    for copy in copies[:3]:
        copy.wait()
    normed[...] = scaled(tokens_in[...].astype(F32), inv_rms_in[...], gain_in[...])
    copies[3].wait()
    pair = dot(normed[...], proj_in[...])
    product[...] = (pair[:, :width] * pair[:, width:]).astype(BF16)
    for copy in copies[4:]:
        copy.wait()


def near_kernel(
    devices, product, normed, taps,
    proj_a, rates_b, residues_b, inv_rms_b, gain_b, out_a, out_b, proj,
    total, queries, taps_wide, scale, weights, rise, fall, fade, shares, out_a_in, out_b_in, proj_in,
    values, proj_q, rates, residues, inv_rms, gain, sems,
):
    copies = fetches(
        [
            (proj_a.at[:, : product.shape[1]], proj_q),
            (rates_b, rates),
            (residues_b, residues),
            (inv_rms_b, inv_rms),
            (gain_b, gain),
            (out_a, out_a_in),
            (proj, proj_in),
            (out_b, out_b_in),
        ],
        sems,
    )
    rows, width = product.shape
    modes = rates.shape[0]
    repeat_rows(taps[...].astype(F32), taps_wide)
    values[...] = product[...].astype(F32)
    total[...] = jnp.zeros_like(total)
    tap_sums(values, taps_wide, total, rim=False)
    for copy in copies:
        copy.wait()
    queries[...] = dot(normed[...], proj_q[...])
    scale[...] = spread(inv_rms[...], width) * gain[...]
    rate = rates[...]
    weight = mode_weights(rate, residues[...], float(devices * rows))
    weights[...] = weight
    fade[...] = jnp.exp(rate * -float(SUB))
    step = lax.broadcasted_iota(jnp.int32, (SUB, width), 0).astype(F32)
    for m in range(modes):
        rise[m] = jnp.exp(-rate[m : m + 1] * step)
        fall[m] = jnp.exp(-rate[m : m + 1] * (SUB - 1.0 - step))
    me = lax.axis_index("seq")
    weight = weight * jnp.exp(-rate)
    for i, (weighted, count, keep) in enumerate(share_plan(me, devices, rows)):
        share = jnp.exp(-rate * jnp.maximum(count, 0).astype(F32))
        shares[i] = jnp.where(keep, share * weight if weighted else share, 0.0)


def middle_kernel(
    near, rim_pair, rim_chain, taps, queries, out_a, tokens, scale, proj, fade, fall,
    partial, signal, normed_b, state, values, total,
):
    width = near.shape[1]
    modes = fade.shape[0]
    me = lax.axis_index("seq")
    total[...] = near[...]
    rim = jnp.where(me % 2 == 1, rim_pair[...].astype(F32), rim_chain[...].astype(F32))
    values[...] = jnp.where(me == 0, 0.0, rim)
    tap_sums(values, taps, total, rim=True)
    gated = (queries[...] * total[...]).astype(BF16)
    term = dot(gated, out_a[...]).astype(BF16)
    partial[...] = term
    hidden = (tokens[...].astype(F32) + term.astype(F32)).astype(BF16)
    normed = (hidden.astype(F32) * scale[...]).astype(BF16)
    normed_b[...] = normed
    pair = dot(normed, proj[:, width:])
    mixed = (pair[:, :width] * pair[:, width:]).astype(BF16).astype(F32)
    signal[...] = mixed
    for lane in range(0, width, LANES):
        here = slice(lane, lane + LANES)
        for m in range(modes):
            drop = fade[m : m + 1, here]
            held = mixed[:SUB, here]
            for row in range(SUB, mixed.shape[0], SUB):
                held = held * drop + mixed[row : row + SUB, here]
            state[m : m + 1, here] = jnp.sum(held * fall[m, :, here], 0, keepdims=True)


def local_kernel(
    signal, weights, rise, fade, normed, proj, partial,
    total, queries, partial_out, response, wide, sems,
):
    copies = fetches([(partial, partial_out)], sems)
    rows, width = signal.shape
    modes = fade.shape[0]
    for lane in range(0, width, LANES):
        here = slice(lane, lane + LANES)
        sums = [jnp.zeros((SUB, LANES), F32)] * (rows // SUB)
        for m in range(modes):
            add_fading(sums, weights[m : m + 1, here] * rise[m, :, here], fade[m : m + 1, here])
        for i, part in enumerate(sums):
            response[i * SUB : (i + 1) * SUB, here] = part
    repeat_rows(response[...], wide)
    total[...] = jnp.zeros_like(total)
    tap_sums(signal, wide, total, rim=False)
    queries[...] = dot(normed[...], proj[:, :width])
    for copy in copies:
        copy.wait()


def add_fading(sums, held, drop):
    for i in range(len(sums)):
        sums[i] = sums[i] + held
        if i + 1 < len(sums):
            held = held * drop


def last_kernel(near, carry, rise, fade, queries, out_b, partial, held, sems):
    rows, width = near.shape
    modes = fade.shape[0]
    columns = []
    for lane in range(0, width, LANES):
        here = slice(lane, lane + LANES)
        sums = [near[row : row + SUB, here] for row in range(0, rows, SUB)]
        for m in range(modes):
            add_fading(sums, carry[m : m + 1, here] * rise[m, :, here], fade[m : m + 1, here])
        columns.append(jnp.concatenate(sums, 0))
    long_out = jnp.concatenate(columns, 1).astype(BF16).astype(F32)
    gated = (queries[...] * long_out).astype(BF16)
    held[...] = dot(gated, out_b[...]).astype(BF16)
    for copy in fetches([(held, partial)], sems):
        copy.wait()


def mode_weights(rates, residues, length):
    energy = one_less_exp(2.0 * rates) / one_less_exp(2.0 * rates * length)
    return residues * jnp.sqrt(energy)


def one_less_exp(value):
    series = jnp.ones_like(value)
    for n in range(9, 1, -1):
        series = 1.0 - value * (1.0 / n) * series
    return jnp.where(value < 0.25, value * series, 1.0 - jnp.exp(-value))


def levels(devices):
    found, stride = [], 2
    while stride < devices:
        radix = max(r for r in (2, 4, 8) if devices // stride % r == 0)
        found.append((stride, radix))
        stride *= radix
    assert stride == devices
    return found


def routes(radix):
    return {8: [(5, 4), (7, 6), (3, 2)], 4: [(3, 2)], 2: []}[radix] + [(1, 1)]


def share_plan(me, devices, rows):
    core = me % 2
    yes = me >= 0
    plan = [(False, (1 - core) * rows, yes), (False, core * rows, yes)]
    for stride, radix in levels(devices):
        place = me // stride % radix
        inner = me % stride // 2 * 2
        for even, odd in routes(radix):
            other = place ^ jnp.where(core == 0, odd, even)
            gap = ((place - 1 - other) * stride + inner) * rows
            plan.append((False, gap, other < place))
            if stride * radix < devices:
                plan.append((False, (radix - 1 - other) * stride * rows, yes))
        if stride * radix < devices:
            plan.append((False, (radix - 1 - place) * stride * rows, yes))
    return plan + [(True, core * rows, yes), (True, 0 * core, core == 1)]


def swap(block, devices, mask):
    return lax.ppermute(block, "seq", [(i, i ^ mask) for i in range(devices)])


def chain(block, devices):
    route = [(i, i + 1) for i in range(1, devices - 1, 2)]
    if devices < 8:
        free = [*range(0, devices, 2), devices - 1]
        route += list(zip(free, [0, *range(1, devices, 2)]))
    else:
        route += [(i, i - 1) for i in range(4, devices - 2, 2)]
        route += [(0, 1), (2, 0), (devices - 2, devices - 1), (devices - 1, devices - 3)]
    return lax.ppermute(block, "seq", route)


def cross(block, devices, stride, radix, even, odd):
    route = []
    for i in range(devices):
        mask = (even, odd)[i % 2]
        place = i // stride % radix
        short = stride * radix == devices and mask & 6 == 6 and place & 4
        route.append((i, i ^ ((mask ^ 2 if short else mask) * stride + 1)))
    return lax.ppermute(block, "seq", route)


def carry_in(state, shares, near, devices):
    share = iter([shares[i] for i in range(shares.shape[0])])
    beside = swap(state, devices, 1)
    total = state * next(share) + beside * next(share)
    halves, wholes = [], []
    for stride, radix in levels(devices):
        last = stride * radix == devices
        half_totals, whole_totals = [], []
        pairs = routes(radix)
        parts = [cross(total, devices, stride, radix, even, odd) for even, odd in pairs]
        for part, (even, odd) in zip(parts, pairs):
            (wholes if even == odd else halves).append(part * next(share))
            if not last:
                (whole_totals if even == odd else half_totals).append(part * next(share))
        if not last:
            whole_totals.append(total * next(share))
            total = functools.reduce(jnp.add, whole_totals)
            if half_totals:
                half = functools.reduce(jnp.add, half_totals)
                total = total + half + swap(half, devices, 1)
    if halves:
        half, near = lax.optimization_barrier((functools.reduce(jnp.add, halves[::-1]), near))
        wholes = [half, swap(half, devices, 1)] + wholes
    before = functools.reduce(jnp.add, wholes)
    return before * next(share) + beside * next(share), near


def on_device(
    tokens,
    inv_rms_a,
    gain_a,
    proj_a,
    taps_a,
    out_a,
    inv_rms_b,
    gain_b,
    proj_b,
    rates_b,
    residues_b,
    out_b,
):
    rows, width = tokens.shape
    taps = taps_a.shape[0]
    modes = rates_b.shape[0]
    devices = lax.axis_size("seq")
    assert taps == rows and rows % SUB == 0 and devices > 2
    wide = pltpu.VMEM((rows, width), F32)
    narrow = pltpu.VMEM((rows, width), BF16)
    square = pltpu.VMEM((width, width), BF16)
    bank = pltpu.VMEM((modes, SUB, width), F32)
    states = pltpu.VMEM((modes, width), F32)
    by_token = pltpu.VMEM((1, rows), F32)
    by_channel = pltpu.VMEM((1, width), F32)
    spread_taps = pltpu.VMEM((taps, SUB, width), F32)
    semaphores = pltpu.SemaphoreType.DMA

    product, normed, tokens, taps_a = call(
        first_kernel,
        (narrow, narrow, narrow, pltpu.VMEM(taps_a.shape, BF16)),
        (pltpu.VMEM((width, 2 * width), BF16), by_token, by_channel, semaphores((5,))),
        [tokens], [inv_rms_a[None]], [gain_a[None]], [proj_a], [taps_a],
    )
    rim_chain = chain(product, devices)
    rim_pair = swap(product, devices, 1)

    shares = pltpu.VMEM((len(share_plan(0, devices, rows)), modes, width), F32)
    (
        near, queries, taps_wide, scale, weights, rise, fall, fade, shares, out_a, out_b, proj_b,
    ) = call(
        functools.partial(near_kernel, devices),
        (
            wide, wide, spread_taps, wide, states, bank, bank, states, shares,
            square, square, pltpu.VMEM(proj_b.shape, BF16),
        ),
        (wide, square, states, states, by_token, by_channel, semaphores((8,))),
        product, normed, taps_a, [proj_a], [rates_b], [residues_b], [inv_rms_b[None]],
        [gain_b[None]], [out_a], [out_b], [proj_b],
    )

    partial_a, signal, normed_b, state = call(
        middle_kernel, (narrow, wide, narrow, states), (wide, wide),
        near, rim_pair, rim_chain, taps_wide, queries, out_a, tokens, scale, proj_b, fade, fall,
    )
    def local(signal):
        return call(
            local_kernel,
            (wide, wide, pltpu.HBM((rows, width), BF16)),
            (wide, spread_taps, semaphores((1,))),
            signal, weights, rise, fade, normed_b, proj_b, partial_a,
        )

    near_b, queries_b, partial_a = local(signal)
    carry, near_b = carry_in(state, shares, near_b, devices)
    (partial_b,) = call(
        last_kernel, (pltpu.HBM((rows, width), BF16),), (narrow, semaphores((1,))),
        near_b, carry, rise, fade, queries_b, out_b,
    )
    return (partial_a, partial_b)


def solution(mesh):
    placed = (
        P(("groups", "seq"), None),
        P(("groups", "seq")),
        P(),
        P(),
        P(),
        P(),
        P(("groups", "seq")),
        P(),
        P(),
        P(),
        P(),
        P(),
    )
    return jax.shard_map(
        on_device,
        mesh=mesh,
        in_specs=placed,
        out_specs=(P(("groups", "seq"), None), P(("groups", "seq"), None)),
        check_vma=False,
    )
```

```python
import functools

import jax
import jax.numpy as jnp
from jax import lax
from jax.experimental import pallas as pl
from jax.experimental.pallas import tpu as pltpu
from jax.sharding import PartitionSpec as P

F32 = jnp.float32
BF16 = jnp.bfloat16
LANES = 128
SUB = 8
TILE_GROUP = 4
VMEM_LIMIT = 32 * 1024 * 1024
WORK = 4 * 1024 * 1024


def call(kernel, outs, scratch, *arrays):
    spaces = [pltpu.HBM if isinstance(a, list) else pltpu.VMEM for a in arrays]
    placed = [
        pltpu.with_memory_space_constraint(a[0], pltpu.HBM) if isinstance(a, list) else a
        for a in arrays
    ]
    return pl.pallas_call(
        kernel,
        out_shape=outs,
        in_specs=[pl.BlockSpec(memory_space=space) for space in spaces],
        out_specs=[pl.BlockSpec(memory_space=out.memory_space) for out in outs],
        scratch_shapes=list(scratch),
        compiler_params=pltpu.CompilerParams(vmem_limit_bytes=VMEM_LIMIT),
        cost_estimate=pl.CostEstimate(flops=0, bytes_accessed=WORK, transcendentals=0),
    )(*placed)


def spread(scales, width):
    rows = scales.shape[1]
    square = jnp.transpose(jnp.broadcast_to(scales, (LANES, rows)))
    return jnp.concatenate([square] * (width // LANES), 1)


def scaled(values, scales, gain):
    return (values * spread(scales, values.shape[1]) * gain).astype(BF16)


def dot(left, right):
    return jnp.dot(left, right, preferred_element_type=F32)


def repeat_rows(taps, wide):
    for j in range(taps.shape[0]):
        wide[j] = jnp.broadcast_to(taps[j : j + 1, :], wide.shape[1:])


def tap_sums(values, wide, total, rim):
    rows, width = values.shape
    tiles = rows // SUB
    row_ids = lax.broadcasted_iota(jnp.int32, (SUB, LANES), 0)
    start = -1 if rim else 0

    def column(at, carried):
        here = pl.ds(at * LANES, LANES)
        above = None
        for first in range(start, start + tiles, TILE_GROUP):
            places = range(first, min(first + TILE_GROUP, start + tiles))
            sums = {}
            for q in range(tiles):
                used = [a for a in places if (q > a if rim else q <= a)]
                if not used:
                    continue
                taps = [wide[q * SUB + r, :, here] for r in range(SUB)]
                for a in used:
                    tile = (tiles if rim else 0) + a - q
                    value = values[tile * SUB : (tile + 1) * SUB, here]
                    terms = [tap * value for tap in taps]
                    old = sums.get(a)
                    sums[a] = terms if old is None else [x + y for x, y in zip(old, terms)]
            for a in places:
                turned = sums[a][:1]
                turned += [pltpu.roll(sums[a][r], r, 0) for r in range(1, SUB)]
                if a >= 0:
                    add_tile(a, here, turned, above)
                above = turned
        if rim:
            add_tile(tiles - 1, here, None, above)
        return carried

    def add_tile(a, here, turned, above):
        parts = [] if turned is None else turned[:1]
        for r in range(1, SUB):
            low = 0.0 if turned is None else turned[r]
            high = 0.0 if above is None else above[r]
            parts.append(jnp.where(row_ids < r, high, low))
        while len(parts) > 1:
            parts = [functools.reduce(jnp.add, parts[i : i + 2]) for i in range(0, len(parts), 2)]
        total[a * SUB : (a + 1) * SUB, here] += parts[0]

    for at in range(width // LANES):
        column(at, 0)


def fetches(pairs, sems):
    copies = [pltpu.make_async_copy(a, b, sems.at[i]) for i, (a, b) in enumerate(pairs)]
    for copy in copies:
        copy.start()
    return copies


def first_kernel(
    tokens, inv_rms, gain, proj, taps, rates, residues, inv_rms_b, gain_b,
    product, normed, tokens_in, proj_q, taps_in, rates_in, residues_in, inv_rms_b_in, gain_b_in,
    proj_in, inv_rms_in, gain_in, sems,
):
    width = tokens.shape[1]
    copies = fetches(
        [
            (tokens, tokens_in),
            (inv_rms, inv_rms_in),
            (gain, gain_in),
            (proj.at[:, width:], proj_in),
            (proj.at[:, :width], proj_q),
            (taps, taps_in),
            (rates, rates_in),
            (residues, residues_in),
            (inv_rms_b, inv_rms_b_in),
            (gain_b, gain_b_in),
        ],
        sems,
    )
    for copy in copies[:3]:
        copy.wait()
    normed[...] = scaled(tokens_in[...].astype(F32), inv_rms_in[...], gain_in[...])
    copies[3].wait()
    pair = dot(normed[...], proj_in[...])
    product[...] = (pair[:, :width] * pair[:, width:]).astype(BF16)
    for copy in copies[4:]:
        copy.wait()


def near_kernel(
    devices, product, normed, proj_q, taps, rates, residues, inv_rms, gain, out_a, out_b, proj,
    total, queries, taps_wide, scale, weights, rise, fall, fade, shares, out_a_in, out_b_in, proj_in,
    values, sems,
):
    copies = fetches([(out_a, out_a_in), (proj, proj_in), (out_b, out_b_in)], sems)
    rows, width = product.shape
    modes = rates.shape[0]
    repeat_rows(taps[...].astype(F32), taps_wide)
    values[...] = product[...].astype(F32)
    total[...] = jnp.zeros_like(total)
    tap_sums(values, taps_wide, total, rim=False)
    queries[...] = dot(normed[...], proj_q[...])
    scale[...] = spread(inv_rms[...], width) * gain[...]
    rate = rates[...]
    weight = mode_weights(rate, residues[...], float(devices * rows))
    weights[...] = weight
    fade[...] = jnp.exp(rate * -float(SUB))
    step = lax.broadcasted_iota(jnp.int32, (SUB, width), 0).astype(F32)
    for m in range(modes):
        rise[m] = jnp.exp(-rate[m : m + 1] * step)
        fall[m] = jnp.exp(-rate[m : m + 1] * (SUB - 1.0 - step))
    me = lax.axis_index("seq")
    weight = weight * jnp.exp(-rate)
    for i, (weighted, count, keep) in enumerate(share_plan(me, devices, rows)):
        share = jnp.exp(-rate * jnp.maximum(count, 0).astype(F32))
        shares[i] = jnp.where(keep, share * weight if weighted else share, 0.0)
    for copy in copies:
        copy.wait()


def middle_kernel(
    near, rim_chain, rim_pair, taps, queries, out_a, tokens, scale, proj, fade, fall,
    partial, signal, normed_b, state, values, total,
):
    width = near.shape[1]
    modes = fade.shape[0]
    me = lax.axis_index("seq")
    total[...] = near[...]
    rim = jnp.where(me % 2 == 1, rim_pair[...].astype(F32), rim_chain[...].astype(F32))
    values[...] = jnp.where(me == 0, 0.0, rim)
    tap_sums(values, taps, total, rim=True)
    gated = (queries[...] * total[...]).astype(BF16)
    term = dot(gated, out_a[...]).astype(BF16)
    partial[...] = term
    hidden = (tokens[...].astype(F32) + term.astype(F32)).astype(BF16)
    normed = (hidden.astype(F32) * scale[...]).astype(BF16)
    normed_b[...] = normed
    pair = dot(normed, proj[:, width:])
    mixed = (pair[:, :width] * pair[:, width:]).astype(BF16).astype(F32)
    signal[...] = mixed
    for lane in range(0, width, LANES):
        here = slice(lane, lane + LANES)
        for m in range(modes):
            drop = fade[m : m + 1, here]
            held = mixed[:SUB, here]
            for row in range(SUB, mixed.shape[0], SUB):
                held = held * drop + mixed[row : row + SUB, here]
            state[m : m + 1, here] = jnp.sum(held * fall[m, :, here], 0, keepdims=True)


def local_kernel(
    signal, weights, rise, fade, normed, proj, partial,
    total, queries, partial_out, response, wide, sems,
):
    copies = fetches([(partial, partial_out)], sems)
    rows, width = signal.shape
    modes = fade.shape[0]
    for lane in range(0, width, LANES):
        here = slice(lane, lane + LANES)
        sums = [jnp.zeros((SUB, LANES), F32)] * (rows // SUB)
        for m in range(modes):
            add_fading(sums, weights[m : m + 1, here] * rise[m, :, here], fade[m : m + 1, here])
        for i, part in enumerate(sums):
            response[i * SUB : (i + 1) * SUB, here] = part
    repeat_rows(response[...], wide)
    total[...] = jnp.zeros_like(total)
    tap_sums(signal, wide, total, rim=False)
    queries[...] = dot(normed[...], proj[:, :width])
    for copy in copies:
        copy.wait()


def add_fading(sums, held, drop):
    for i in range(len(sums)):
        sums[i] = sums[i] + held
        if i + 1 < len(sums):
            held = held * drop


def last_kernel(near, carry, rise, fade, queries, out_b, partial, held, sems):
    rows, width = near.shape
    modes = fade.shape[0]
    columns = []
    for lane in range(0, width, LANES):
        here = slice(lane, lane + LANES)
        sums = [near[row : row + SUB, here] for row in range(0, rows, SUB)]
        for m in range(modes):
            add_fading(sums, carry[m : m + 1, here] * rise[m, :, here], fade[m : m + 1, here])
        columns.append(jnp.concatenate(sums, 0))
    long_out = jnp.concatenate(columns, 1).astype(BF16).astype(F32)
    gated = (queries[...] * long_out).astype(BF16)
    held[...] = dot(gated, out_b[...]).astype(BF16)
    for copy in fetches([(held, partial)], sems):
        copy.wait()


def mode_weights(rates, residues, length):
    energy = one_less_exp(2.0 * rates) / one_less_exp(2.0 * rates * length)
    return residues * jnp.sqrt(energy)


def one_less_exp(value):
    series = jnp.ones_like(value)
    for n in range(9, 1, -1):
        series = 1.0 - value * (1.0 / n) * series
    return jnp.where(value < 0.25, value * series, 1.0 - jnp.exp(-value))


def levels(devices):
    found, stride = [], 2
    while stride < devices:
        radix = 4 if stride == 2 else max(r for r in (2, 4, 8) if devices // stride % r == 0)
        found.append((stride, radix))
        stride *= radix
    assert stride == devices
    return found


def routes(radix):
    nearest = [(1, 1)]
    return {8: [(5, 4), (7, 6), (3, 2)] + nearest, 4: nearest + [(3, 2)], 2: nearest}[radix]


def share_plan(me, devices, rows):
    core = me % 2
    yes = me >= 0
    plan = [(False, (1 - core) * rows, yes), (False, core * rows, yes)]
    for stride, radix in levels(devices):
        place = me // stride % radix
        inner = me % stride // 2 * 2
        for even, odd in routes(radix):
            other = place ^ jnp.where(core == 0, odd, even)
            gap = ((place - 1 - other) * stride + inner) * rows
            plan.append((False, gap, other < place))
            if stride * radix < devices:
                plan.append((False, (radix - 1 - other) * stride * rows, yes))
        if stride * radix < devices:
            plan.append((False, (radix - 1 - place) * stride * rows, yes))
    return plan + [(True, core * rows, yes), (True, 0 * core, core == 1)]


def swap(block, devices, mask):
    return lax.ppermute(block, "seq", [(i, i ^ mask) for i in range(devices)])


def chain(block, devices):
    route = [(i, i + 1) for i in range(1, devices - 1, 2)]
    if devices < 8:
        free = [*range(0, devices, 2), devices - 1]
        route += list(zip(free, [0, *range(1, devices, 2)]))
    else:
        route += [(i, i - 1) for i in range(4, devices - 2, 2)]
        route += [(0, 1), (2, 0), (devices - 2, devices - 1), (devices - 1, devices - 3)]
    return lax.ppermute(block, "seq", route)


def cross(block, devices, stride, radix, even, odd):
    route = []
    for i in range(devices):
        mask = (even, odd)[i % 2]
        place = i // stride % radix
        short = stride * radix == devices and mask & 6 == 6 and place & 4
        route.append((i, i ^ ((mask ^ 2 if short else mask) * stride + 1)))
    return lax.ppermute(block, "seq", route)


def carry_in(state, shares, near, devices):
    share = iter([shares[i] for i in range(shares.shape[0])])
    beside = swap(state, devices, 1)
    total = state * next(share) + beside * next(share)
    halves, wholes = [], []
    for stride, radix in levels(devices):
        last = stride * radix == devices
        half_totals, whole_totals = [], []
        pairs = routes(radix)
        parts = [cross(total, devices, stride, radix, even, odd) for even, odd in pairs]
        for part, (even, odd) in zip(parts, pairs):
            (wholes if even == odd else halves).append(part * next(share))
            if not last:
                (whole_totals if even == odd else half_totals).append(part * next(share))
        if not last:
            whole_totals.append(total * next(share))
            total = functools.reduce(jnp.add, whole_totals)
            if half_totals:
                half = functools.reduce(jnp.add, half_totals)
                total = total + half + swap(half, devices, 1)
    if halves:
        half, near = lax.optimization_barrier((functools.reduce(jnp.add, halves), near))
        wholes = [half, swap(half, devices, 1)] + wholes
    before = functools.reduce(jnp.add, wholes)
    return before * next(share) + beside * next(share), near


def on_device(
    tokens,
    inv_rms_a,
    gain_a,
    proj_a,
    taps_a,
    out_a,
    inv_rms_b,
    gain_b,
    proj_b,
    rates_b,
    residues_b,
    out_b,
):
    rows, width = tokens.shape
    taps = taps_a.shape[0]
    modes = rates_b.shape[0]
    devices = lax.axis_size("seq")
    assert taps == rows and rows % SUB == 0 and devices > 2
    wide = pltpu.VMEM((rows, width), F32)
    narrow = pltpu.VMEM((rows, width), BF16)
    square = pltpu.VMEM((width, width), BF16)
    bank = pltpu.VMEM((modes, SUB, width), F32)
    states = pltpu.VMEM((modes, width), F32)
    by_token = pltpu.VMEM((1, rows), F32)
    by_channel = pltpu.VMEM((1, width), F32)
    spread_taps = pltpu.VMEM((taps, SUB, width), F32)
    semaphores = pltpu.SemaphoreType.DMA

    product, normed, tokens, proj_q, taps_a, rates, residues, inv_rms, gain = call(
        first_kernel,
        (narrow, narrow, narrow, square, narrow, states, states, by_token, by_channel),
        (pltpu.VMEM((width, 2 * width), BF16), by_token, by_channel, semaphores((10,))),
        [tokens], [inv_rms_a[None]], [gain_a[None]], [proj_a], [taps_a], [rates_b], [residues_b],
        [inv_rms_b[None]], [gain_b[None]],
    )
    rim_chain = chain(product, devices)
    rim_pair = swap(product, devices, 1)

    shares = pltpu.VMEM((len(share_plan(0, devices, rows)), modes, width), F32)
    (
        near, queries, taps_wide, scale, weights, rise, fall, fade, shares, out_a, out_b, proj_b,
    ) = call(
        functools.partial(near_kernel, devices),
        (
            wide, wide, spread_taps, wide, states, bank, bank, states, shares,
            square, square, pltpu.VMEM(proj_b.shape, BF16),
        ),
        (wide, semaphores((3,))),
        product, normed, proj_q, taps_a, rates, residues, inv_rms, gain, [out_a], [out_b], [proj_b],
    )

    partial_a, signal, normed_b, state = call(
        middle_kernel, (narrow, wide, narrow, states), (wide, wide),
        near, rim_chain, rim_pair, taps_wide, queries, out_a, tokens, scale, proj_b, fade, fall,
    )
    near_b, queries_b, partial_a = call(
        local_kernel,
        (wide, wide, pltpu.HBM((rows, width), BF16)),
        (wide, spread_taps, semaphores((1,))),
        signal, weights, rise, fade, normed_b, proj_b, partial_a,
    )
    carry, near_b = carry_in(state, shares, near_b, devices)
    (partial_b,) = call(
        last_kernel, (pltpu.HBM((rows, width), BF16),), (narrow, semaphores((1,))),
        near_b, carry, rise, fade, queries_b, out_b,
    )
    return (partial_a, partial_b)


def solution(mesh):
    placed = (
        P(("groups", "seq"), None),
        P(("groups", "seq")),
        P(),
        P(),
        P(),
        P(),
        P(("groups", "seq")),
        P(),
        P(),
        P(),
        P(),
        P(),
    )
    return jax.shard_map(
        on_device,
        mesh=mesh,
        in_specs=placed,
        out_specs=(P(("groups", "seq"), None), P(("groups", "seq"), None)),
        check_vma=False,
    )
```
